32 devices in a mesh: rep: 2 (over y), tp: 4 (over z), ad: 2 (over x), sub: 2 (over core).
Axes of the slice: x: 2, y: 2, z: 4, core: 2. Of those that a mesh axis runs over, the one named last changes fastest.
Arguments:
- tokens: bfloat16 [4, 512, 8192], P(('rep', 'ad'), None, 'tp'), parts along dimension 0, may hold values from -6 to 6
- query_weight_matrix: bfloat16 [8192, 4096], P('tp', 'sub'), may hold values from -0.0625 to 0.0625
- adapter_down_weight: bfloat16 [24, 16, 8192], P('ad', None, 'tp'), may hold values from -0.0625 to 0.0625
- adapter_up_weight: bfloat16 [24, 16, 4096], P('ad', None, 'sub'), may hold values from -0.75 to 0.75
- request_adapter_id: int32 [4, 8], P('rep'), parts along dimension 0, may hold values from 0 to 23, as said below
- request_token_length: int32 [4, 8], P(('rep', 'ad')), parts along dimension 0, may hold values from 1 to 256, 512 in all within a row
- adapter_store_slot: int32 [48], P('rep'), parts along dimension 0, may hold values from 0 to 23, as said below
Outputs:
- query: bfloat16 [4, 512, 4096], P(('rep', 'ad'), 'tp', 'sub'), parts along dimension 0
The draws below stay inside these ranges and needn't reach their ends.
There are 2 independent parts, one for each index of `rep`. The reference program is written for one: setup_inputs(seed, part) draws one part's arguments, and reference() takes and returns one part's arrays. A program takes and returns all parts, laid end to end along the dimension named above; an argument that names none is the same for every part. Nothing has to cross between parts.
Inputs may be any that keep to these rules, and one draw needn't show every extreme that they name: `request_adapter_id`: among the 8 requests of one group, at most 4 use adapters whose slot lies on one index of ad (slot // 12); in every group exactly 4 use one such index, a different one from group to group. A permutation: adapter a is row adapter_store_slot[a] of the store, held by index adapter_store_slot[a] // 12 of ad.
All inputs are finite; a program needn't handle non-finite values.
Results may differ from the reference program's by a relative error of at most 0.013.
Values may be sent and summed in bfloat16 or wider, within the bound.
A program may use at most 64 MiB of HBM per device.

```python
import math
import jax
import jax.numpy as jnp
import numpy as np
from jax import lax

MODEL_WIDTH = 8192
QUERY_WIDTH = 4096
ADAPTER_RANK = 16
TOK_AD = 512
REQUEST_COUNT = 8
CAP = 4
ADP = 12
GROUPS = 2
ADAPTER_COUNT = 24
MOST_LEN = 256
N_TP = 4


def shared_slots(key):
    return jax.random.permutation(jax.random.fold_in(key, 11), ADAPTER_COUNT).astype(jnp.int32)


def draw_adapter_store_slot(key, part):
    slot_perm = shared_slots(key)
    return slot_perm


def draw_request_adapter_id(key, part):
    slot_perm = shared_slots(key)
    key = jax.random.fold_in(key, 5)
    adapter_at = jnp.argsort(slot_perm).astype(jnp.int32)
    hot_owners = jax.random.permutation(jax.random.fold_in(key, 7), GROUPS).astype(jnp.int32)

    def one_group(group_key, hot_owner):
        keys = jax.random.split(group_key, 4)
        others = jnp.repeat(jnp.arange(GROUPS - 1, dtype=jnp.int32), CAP)
        others = others + (others >= hot_owner).astype(jnp.int32)
        others = jax.random.permutation(keys[1], others)[:REQUEST_COUNT - CAP]
        owner_list = jnp.concatenate([jnp.full((CAP,), hot_owner, jnp.int32), others])
        owner_list = jax.random.permutation(keys[2], owner_list)
        within = jax.random.randint(keys[3], (REQUEST_COUNT,), 0, ADP).astype(jnp.int32)
        return adapter_at[owner_list * ADP + within]
    return jax.vmap(one_group)(jax.random.split(key, GROUPS), hot_owners)


def block_levels(key, shape, pieces, low, high):
    factor_of = 1.0
    for axis_at, shards_of in pieces:
        steps = jax.random.uniform(jax.random.fold_in(jax.random.fold_in(key, 6), axis_at), (shards_of,), jnp.float32, low / len(pieces), high / len(pieces))
        factor_of = factor_of * jnp.repeat(jnp.exp(steps), shape[axis_at] // shards_of).reshape((-1,) + (1,) * (len(shape) - 1 - axis_at))
    return factor_of


def profile(number_of, total, reach, lean):
    weights = [(1 << 20) // math.isqrt(rank ** lean) + 1 for rank in range(2, number_of + 1)]
    spare, given = total - reach - (number_of - 1), [1] * (number_of - 1)
    while spare > 0:
        candidates = [i for i in range(number_of - 1) if given[i] < reach]
        whole, budget = sum([weights[i] for i in candidates]), spare
        for i in candidates:
            extra = min(reach - given[i], max(1, budget * weights[i] // whole), spare)
            given[i] = given[i] + extra
            spare = spare - extra
    return np.array([reach] + given)


def ragged(key, number_of, total, most, lean):
    if number_of == 2:
        one = jax.random.randint(key, (), max(1, total - most), min(most, total - 1) + 1)
        return jnp.stack([one, total - one])
    tallies = jnp.asarray(profile(number_of, total, most, lean), jnp.int32)
    couples = (number_of - 1) // 2
    donor, taker = tallies[1:1 + 2 * couples:2], tallies[2:2 + 2 * couples:2]
    margin = jnp.minimum(donor - 1, most - taker)
    moved = jax.random.randint(jax.random.fold_in(key, 1), (couples,), 0, 1 << 20) % (margin + 1)
    tallies = tallies.at[1:1 + 2 * couples:2].set(donor - moved).at[2:2 + 2 * couples:2].set(taker + moved)
    return tallies[jax.random.permutation(jax.random.fold_in(key, 2), number_of)]


def scatter_about(rng, extent, spread, most, shards=(), held_as=jnp.bfloat16):
    entries = jax.random.normal(rng, extent, jnp.float32) * spread
    if len(shards) > 0:
        entries = block_levels(rng, extent, shards, -0.22, 0.18) * entries
    return jnp.clip(entries, min=-most, max=most).astype(held_as)


def setup_inputs(seed: int = 0, part: int = 0) -> dict:
    key_of = jax.random.split(jax.random.key(seed), 8)
    own_keys = jax.random.split(jax.random.fold_in(key_of[7], part), 8)
    return {
        "tokens": scatter_about(own_keys[0], (GROUPS, TOK_AD, MODEL_WIDTH), 1.0, 6.0, ((0, 2), (2, 4))),
        "query_weight_matrix": scatter_about(key_of[1], (MODEL_WIDTH, QUERY_WIDTH), MODEL_WIDTH ** -0.5, 0.0625, ((0, 4), (1, 2))),
        "adapter_down_weight": scatter_about(key_of[2], (ADAPTER_COUNT, ADAPTER_RANK, MODEL_WIDTH), MODEL_WIDTH ** -0.5, 0.0625, ((0, 2), (2, 4))),
        "adapter_up_weight": scatter_about(key_of[3], (ADAPTER_COUNT, ADAPTER_RANK, QUERY_WIDTH), (4 * ADAPTER_RANK) ** -0.5, 0.75, ((0, 2), (2, 2))),
        "request_adapter_id": draw_request_adapter_id(jax.random.fold_in(jax.random.fold_in(key_of[7], part), 71), part),
        "request_token_length": jax.vmap(lambda own: ragged(own, REQUEST_COUNT, TOK_AD, MOST_LEN, 2))(jax.random.split(own_keys[5], GROUPS)).reshape((GROUPS, REQUEST_COUNT)).astype(jnp.int32),
        "adapter_store_slot": draw_adapter_store_slot(jax.random.fold_in(jax.random.fold_in(key_of[7], part), 71), part),
    }


ADAPTER_SCALE = 2.0


def reference(tokens, query_weight_matrix, adapter_down_weight, adapter_up_weight, request_adapter_id, request_token_length, adapter_store_slot):
    width_part = MODEL_WIDTH // N_TP

    def one_group(inputs):
        hidden, request_ids, lengths = inputs
        request_store_slot = adapter_store_slot[request_ids]
        request_down_weight = adapter_down_weight[request_store_slot].reshape(REQUEST_COUNT * ADAPTER_RANK, MODEL_WIDTH)
        request_up_weight = adapter_up_weight[request_store_slot].reshape(REQUEST_COUNT * ADAPTER_RANK, QUERY_WIDTH)
        seg_ends = jnp.cumsum(lengths).astype(jnp.int32)
        seg_starts = seg_ends - lengths
        positions = jnp.arange(TOK_AD, dtype=jnp.int32)
        token_mask = ((positions[:, None] >= seg_starts[None, :]) & (positions[:, None] < seg_ends[None, :])).astype(jnp.float32)
        down_acts = jnp.dot(hidden, request_down_weight.T, preferred_element_type=jnp.float32).reshape(TOK_AD, REQUEST_COUNT, ADAPTER_RANK)
        rank_acts = jnp.sum(token_mask[:, :, None] * down_acts, axis=1).astype(jnp.bfloat16)
        expanded_rows = (token_mask[:, :, None] * rank_acts[:, None, :].astype(jnp.float32)).reshape(TOK_AD, REQUEST_COUNT * ADAPTER_RANK).astype(jnp.bfloat16)
        adapter_output = jnp.dot(expanded_rows, request_up_weight, preferred_element_type=jnp.float32)
        base_query_sum = jnp.zeros((TOK_AD, QUERY_WIDTH), jnp.float32)
        for piece in range(N_TP):
            lower = piece * width_part
            partial_term = jnp.dot(hidden[:, lower:lower + width_part], query_weight_matrix[lower:lower + width_part, :], preferred_element_type=jnp.float32).astype(jnp.bfloat16)
            base_query_sum = base_query_sum + lax.optimization_barrier(partial_term).astype(jnp.float32)
        return (base_query_sum + ADAPTER_SCALE * adapter_output).astype(jnp.bfloat16)

    return lax.map(one_group, (tokens, request_adapter_id, request_token_length))
```

```python
import functools
import jax
import jax.numpy as jnp
from jax import lax
from jax.experimental import pallas as pl
from jax.experimental.pallas import tpu as pltpu
from jax.sharding import PartitionSpec as P

CAP = 4

ADAPTER_SCALE = 2.0

BLOCK_COLS = 256
LAG = 2
DEPTH = 3

MESH = pl.DeviceIdType.MESH
F32 = jnp.float32
BF16 = jnp.bfloat16


def one_hot(condition):
    return jnp.where(condition, 1.0, 0.0).astype(BF16)


def kernel(
    tp_count,
    groups,
    rank_extent,
    tokens_hbm,
    weight_hbm,
    down_hbm,
    up_hbm,
    ids_ref,
    lengths_ref,
    slots_ref,
    out_hbm,
    tok,
    weight,
    down,
    up,
    stage,
    from_left,
    from_right,
    down_send,
    up_send,
    got_down,
    got_up,
    rank_send,
    rank_got,
    expanded,
    total,
    out_stage,
    tok_sem,
    weight_sem,
    store_sem,
    flow_send_sem,
    left_sem,
    right_sem,
    adapter_send_sem,
    adapter_recv_sem,
    rank_send_sem,
    rank_recv_sem,
    out_sem,
):
    z = lax.axis_index("tp")
    ad = lax.axis_index("ad")
    rows = tok.shape[1]
    blocks = weight.shape[0]
    requests = ids_ref.shape[1]
    store_rows = down.shape[0]
    held = store_rows // rank_extent
    cap_rows = CAP * rank_extent
    lanes = groups * cap_rows
    rank_bits = rank_extent.bit_length() - 1
    last = tp_count - 1

    def tok_copy(chunk):
        return pltpu.make_async_copy(
            tokens_hbm.at[pl.ds(chunk * rows, rows), :], tok.at[chunk], tok_sem.at[chunk]
        )

    def weight_copy(block):
        return pltpu.make_async_copy(
            weight_hbm.at[:, pl.ds(pl.multiple_of(block * BLOCK_COLS, BLOCK_COLS), BLOCK_COLS)],
            weight.at[block],
            weight_sem.at[block],
        )

    down_copy = pltpu.make_async_copy(down_hbm, down, store_sem.at[0])
    up_copy = pltpu.make_async_copy(up_hbm, up, store_sem.at[1])
    tok_copy(last).start()
    tok_copy(0).start()
    weight_copy(0).start()
    for chunk in range(1, last):
        tok_copy(chunk).start()
    weight_copy(1).start()
    down_copy.start()
    up_copy.start()
    for block in range(2, blocks):
        weight_copy(block).start()

    barrier = pltpu.get_barrier_semaphore()
    for axis, size in (("tp", tp_count), ("ad", groups)):
        for hop in range(1, size):
            other = lax.rem(lax.axis_index(axis) + hop, size)
            pl.semaphore_signal(barrier, inc=1, device_id={axis: other}, device_id_type=MESH)
    pl.semaphore_wait(barrier, tp_count + groups - 2)

    def right_copy(k):
        return pltpu.make_async_remote_copy(
            stage.at[last * blocks - k + 2 * lax.rem(k, blocks)],
            from_left.at[k],
            flow_send_sem.at[last * blocks - k + 2 * lax.rem(k, blocks)],
            left_sem.at[k],
            device_id={"tp": lax.rem(z + 1, tp_count)},
            device_id_type=MESH,
        )

    def left_copy(k):
        return pltpu.make_async_remote_copy(
            stage.at[k],
            from_right.at[k],
            flow_send_sem.at[k],
            right_sem.at[k],
            device_id={"tp": lax.rem(z + last, tp_count)},
            device_id_type=MESH,
        )

    def base_part(chunk, block):
        part = jnp.dot(tok[chunk], weight[block], preferred_element_type=F32)
        return part.astype(BF16)

    def adapter_copy(which, hop):
        send, got = ((down_send, got_down), (up_send, got_up))[which]
        return pltpu.make_async_remote_copy(
            send.at[hop - 1],
            got.at[ad],
            adapter_send_sem.at[which, hop - 1],
            adapter_recv_sem.at[which, hop - 1],
            device_id={"ad": lax.rem(ad + hop, groups)},
            device_id_type=MESH,
        )

    def rank_copy(hop):
        target = lax.rem(z + hop, tp_count)
        return pltpu.make_async_remote_copy(
            rank_send.at[target],
            rank_got.at[hop - 1],
            rank_send_sem.at[hop - 1],
            rank_recv_sem.at[hop - 1],
            device_id={"tp": target},
            device_id_type=MESH,
        )

    def places(group):
        found = []
        for q in range(requests):
            slot = slots_ref[ids_ref[group, q]]
            owner = jnp.int32(0)
            for g in range(1, groups):
                owner = owner + jnp.where(slot >= g * held, 1, 0)
            rank = jnp.int32(0)
            for earlier, _, _ in found:
                rank = rank + jnp.where(earlier == owner, 1, 0)
            found.append((owner, rank, slot - owner * held))
        return found

    def send_adapters():
        down_copy.wait()
        up_copy.wait()
        row = lax.broadcasted_iota(jnp.int32, (cap_rows, store_rows), 0)
        col = lax.broadcasted_iota(jnp.int32, (cap_rows, store_rows), 1)
        for hop in list(range(1, groups)) + [0]:
            wanted = jnp.full((cap_rows, store_rows), -1 - rank_extent, jnp.int32)
            for owner, rank, within in places(lax.rem(ad + hop, groups)):
                place = jnp.where(owner == ad, rank, -1)
                wanted = jnp.where((row >> rank_bits) == place, within * rank_extent, wanted)
            chosen = one_hot(col == wanted + (row & (rank_extent - 1)))
            for which, (store, send, got) in enumerate(
                ((down, down_send, got_down), (up, up_send, got_up))
            ):
                picked = jnp.dot(chosen, store[...], preferred_element_type=F32).astype(BF16)
                if hop > 0:
                    send[hop - 1] = picked
                    adapter_copy(which, hop).start()
                else:
                    got[ad] = picked

    def token_mask(first, count):
        lane = lax.broadcasted_iota(jnp.int32, (1, lanes), 1) >> rank_bits
        starts = jnp.zeros((1, lanes), jnp.int32)
        ends = jnp.zeros((1, lanes), jnp.int32)
        position = jnp.int32(0)
        for q, (owner, rank, _) in enumerate(places(ad)):
            here = lane == owner * CAP + rank
            starts = jnp.where(here, position, starts)
            position = position + lengths_ref[0, q]
            ends = jnp.where(here, position, ends)
        at = first + lax.broadcasted_iota(jnp.int32, (count, lanes), 0)
        return (at >= starts) & (at < ends)

    def rank_hot():
        lane = lax.broadcasted_iota(jnp.int32, (rank_extent, lanes), 1)
        row = lax.broadcasted_iota(jnp.int32, (rank_extent, lanes), 0)
        return one_hot((lane & (rank_extent - 1)) == row)

    def send_ranks():
        for hop in range(1, groups):
            adapter_copy(0, hop).wait()
        acts = lax.dot_general(
            tok[...].reshape(tp_count * rows, -1),
            got_down[...].reshape(lanes, -1),
            (((1,), (1,)), ((), ())),
            preferred_element_type=F32,
        )
        acts = jnp.where(token_mask(0, tp_count * rows), acts, 0.0).astype(BF16)
        for chunk in range(tp_count):
            rank_send[chunk] = lax.dot_general(
                rank_hot(),
                acts[chunk * rows : (chunk + 1) * rows],
                (((1,), (1,)), ((), ())),
                preferred_element_type=F32,
            ).astype(BF16)
        for hop in range(1, tp_count):
            rank_copy(hop).start()

    def expand_ranks():
        for hop in range(1, tp_count):
            rank_copy(hop).wait()
        for hop in range(1, groups):
            adapter_copy(1, hop).wait()
        rank_acts = rank_send[z].astype(F32)
        for hop in range(1, tp_count):
            rank_acts = rank_acts + rank_got[hop - 1].astype(F32)
        spread = lax.dot_general(
            rank_acts.astype(BF16), rank_hot(), (((0,), (0,)), ((), ())), preferred_element_type=F32
        )
        expanded[...] = jnp.where(token_mask(z * rows, rows), spread, 0.0).astype(BF16)

    def out_copy(block):
        return pltpu.make_async_copy(
            out_stage.at[block],
            out_hbm.at[:, pl.ds(pl.multiple_of(block * BLOCK_COLS, BLOCK_COLS), BLOCK_COLS)],
            out_sem.at[block],
        )

    right_count = (last - z) * blocks
    left_count = z * blocks
    final_step = (tp_count - 2) * blocks + LAG

    def step(s, carry):
        @pl.when(s < blocks)
        def _():
            weight_copy(s).wait()

        @pl.when(s == 0)
        def _():
            tok_copy(last).wait()
            tok_copy(0).wait()

        @pl.when(s == 1)
        def _():
            for chunk in range(1, last):
                tok_copy(chunk).wait()

        k_right = s - LAG * z

        @pl.when((k_right >= DEPTH) & (k_right < right_count + DEPTH))
        def _():
            right_copy(k_right - DEPTH).wait_send()

        @pl.when((k_right >= 0) & (k_right < right_count))
        def _():
            chunk = last - k_right // blocks
            block = lax.rem(k_right, blocks)
            at = chunk * blocks + block
            part = base_part(chunk, block)

            @pl.when(z == 0)
            def _():
                stage[at] = part

            @pl.when(z > 0)
            def _():
                right_copy(k_right).wait_recv()
                stage[at] = (part.astype(F32) + from_left[k_right].astype(F32)).astype(BF16)

            right_copy(k_right).start()

        k_left = s - LAG * (last - z)

        @pl.when((k_left >= DEPTH) & (k_left < left_count + DEPTH))
        def _():
            left_copy(k_left - DEPTH).wait_send()

        @pl.when((k_left >= 0) & (k_left < left_count))
        def _():
            part = base_part(k_left // blocks, lax.rem(k_left, blocks))

            @pl.when(z == last)
            def _():
                stage[k_left] = part

            @pl.when(z < last)
            def _():
                left_copy(k_left).wait_recv()
                stage[k_left] = (part.astype(F32) + from_right[k_left].astype(F32)).astype(BF16)

            left_copy(k_left).start()

        @pl.when(s == 2)
        def _():
            send_adapters()

        @pl.when(s == blocks)
        def _():
            send_ranks()

        @pl.when(s == final_step - 2)
        def _():
            expand_ranks()

        block = s - final_step

        @pl.when((block >= 0) & (block < blocks))
        def _():
            cols = pl.ds(pl.multiple_of(block * BLOCK_COLS, BLOCK_COLS), BLOCK_COLS)
            lora = jnp.dot(
                expanded[...],
                got_up[:, :, cols].reshape(lanes, BLOCK_COLS),
                preferred_element_type=F32,
            )
            total[...] = base_part(z, block).astype(F32) + ADAPTER_SCALE * lora

            @pl.when(z < last)
            def _():
                left_copy(left_count + block).wait_recv()
                total[...] += from_right[left_count + block].astype(F32)

            @pl.when(z > 0)
            def _():
                right_copy(right_count + block).wait_recv()
                total[...] += from_left[right_count + block].astype(F32)

            out_stage[block] = total[...].astype(BF16)
            out_copy(block).start()

        return carry

    lax.fori_loop(0, last * blocks + max(LAG, DEPTH), step, 0)
    for block in range(blocks):
        out_copy(block).wait()


def local(
    tokens,
    query_weight_matrix,
    adapter_down_weight,
    adapter_up_weight,
    request_adapter_id,
    request_token_length,
    adapter_store_slot,
):
    tp_count = lax.axis_size("tp")
    groups = lax.axis_size("ad")
    tok_rows, width = tokens.shape[1:]
    cols = query_weight_matrix.shape[1]
    held, rank_extent = adapter_down_weight.shape[:2]
    rows = tok_rows // tp_count
    blocks = cols // BLOCK_COLS
    cap_rows = CAP * rank_extent
    block = (rows, BLOCK_COLS)
    flow = (tp_count - 1) * blocks
    hbm = pl.BlockSpec(memory_space=pl.ANY)
    smem = pl.BlockSpec(memory_space=pltpu.SMEM)
    dma = pltpu.SemaphoreType.DMA
    query = pl.pallas_call(
        functools.partial(kernel, tp_count, groups, rank_extent),
        out_shape=jax.ShapeDtypeStruct((rows, cols), BF16),
        in_specs=[hbm] * 4 + [smem] * 3,
        out_specs=hbm,
        scratch_shapes=[
            pltpu.VMEM((tp_count, rows, width), BF16),
            pltpu.VMEM((blocks, width, BLOCK_COLS), BF16),
            pltpu.VMEM((held * rank_extent, width), BF16),
            pltpu.VMEM((held * rank_extent, cols), BF16),
            pltpu.VMEM((tp_count * blocks, *block), BF16),
            pltpu.VMEM((flow, *block), BF16),
            pltpu.VMEM((flow, *block), BF16),
            pltpu.VMEM((groups - 1, cap_rows, width), BF16),
            pltpu.VMEM((groups - 1, cap_rows, cols), BF16),
            pltpu.VMEM((groups, cap_rows, width), BF16),
            pltpu.VMEM((groups, cap_rows, cols), BF16),
            pltpu.VMEM((tp_count, rank_extent, rows), BF16),
            pltpu.VMEM((tp_count - 1, rank_extent, rows), BF16),
            pltpu.VMEM((rows, groups * cap_rows), BF16),
            pltpu.VMEM(block, F32),
            pltpu.VMEM((blocks, *block), BF16),
            dma((tp_count,)),
            dma((blocks,)),
            dma((2,)),
            dma((tp_count * blocks,)),
            dma((flow,)),
            dma((flow,)),
            dma((2, groups - 1)),
            dma((2, groups - 1)),
            dma((tp_count - 1,)),
            dma((tp_count - 1,)),
            dma((blocks,)),
        ],
        compiler_params=pltpu.CompilerParams(
            collective_id=0, has_side_effects=True, vmem_limit_bytes=56 * 2**20
        ),
        cost_estimate=pl.CostEstimate(
            flops=2 * tok_rows * width * cols,
            bytes_accessed=2 * width * (cols + tok_rows),
            transcendentals=0,
        ),
        name="query_projection",
    )(
        tokens.reshape(tok_rows, width),
        query_weight_matrix,
        adapter_down_weight.reshape(held * rank_extent, width),
        adapter_up_weight.reshape(held * rank_extent, cols),
        request_adapter_id,
        request_token_length,
        adapter_store_slot,
    )
    return query[None]


def solution(mesh):
    return jax.shard_map(
        local,
        mesh=mesh,
        in_specs=(
            P(("rep", "ad"), None, "tp"),
            P("tp", "sub"),
            P("ad", None, "tp"),
            P("ad", None, "sub"),
            P("rep", None),
            P(("rep", "ad"), None),
            P("rep"),
        ),
        out_specs=P(("rep", "ad"), "tp", "sub"),
        check_vma=False,
    )
```

```python
import functools
import jax
import jax.numpy as jnp
from jax import lax
from jax.experimental import pallas as pl
from jax.experimental.pallas import tpu as pltpu
from jax.sharding import PartitionSpec as P

CAP = 4

ADAPTER_SCALE = 2.0

BLOCK_COLS = 512
LAG = 2
DEPTH = 4

MESH = pl.DeviceIdType.MESH
F32 = jnp.float32
BF16 = jnp.bfloat16


def one_hot(condition):
    return jnp.where(condition, 1.0, 0.0).astype(BF16)


def kernel(
    tp_count,
    groups,
    rank_extent,
    tokens_hbm,
    weight_hbm,
    down_hbm,
    up_hbm,
    ids_ref,
    lengths_ref,
    slots_ref,
    out,
    tok,
    weight,
    down,
    up,
    stage,
    from_left,
    from_right,
    down_send,
    up_send,
    got_down,
    got_up,
    rank_own,
    rank_send,
    rank_got,
    rank_sum,
    expanded,
    total,
    tok_sem,
    weight_sem,
    store_sem,
    flow_send_sem,
    left_sem,
    right_sem,
    adapter_send_sem,
    adapter_recv_sem,
    rank_send_sem,
    rank_recv_sem,
):
    z = lax.axis_index("tp")
    ad = lax.axis_index("ad")
    rows = tok.shape[1]
    blocks = weight.shape[0]
    requests = ids_ref.shape[1]
    store_rows = down.shape[0]
    held = store_rows // rank_extent
    cap_rows = CAP * rank_extent
    lanes = groups * cap_rows
    rank_bits = rank_extent.bit_length() - 1
    last = tp_count - 1

    def tok_copy(chunk):
        return pltpu.make_async_copy(
            tokens_hbm.at[pl.ds(chunk * rows, rows), :], tok.at[chunk], tok_sem.at[chunk]
        )

    def weight_copy(block):
        return pltpu.make_async_copy(
            weight_hbm.at[:, pl.ds(pl.multiple_of(block * BLOCK_COLS, BLOCK_COLS), BLOCK_COLS)],
            weight.at[block],
            weight_sem.at[block],
        )

    down_copy = pltpu.make_async_copy(down_hbm, down, store_sem.at[0])
    up_copy = pltpu.make_async_copy(up_hbm, up, store_sem.at[1])
    barrier = pltpu.get_barrier_semaphore()

    def greet(target):
        pl.semaphore_signal(barrier, inc=1, device_id=target, device_id_type=MESH)

    @pl.when(z < last)
    def _():
        greet({"tp": lax.rem(z + 1, tp_count)})

    @pl.when(z > 0)
    def _():
        greet({"tp": lax.rem(z + last, tp_count)})

    for hop in range(1, groups):
        greet({"ad": lax.rem(ad + hop, groups)})

    first = jnp.where(z == last, 0, last)
    tok_copy(first).start()
    weight_copy(0).start()
    weight_copy(1).start()
    tok_copy(last - first).start()
    for chunk in range(1, last):
        tok_copy(chunk).start()
    down_copy.start()
    up_copy.start()
    for block in range(2, blocks):
        weight_copy(block).start()

    def right_copy(k):
        return pltpu.make_async_remote_copy(
            stage.at[last * blocks - k + 2 * lax.rem(k, blocks)],
            from_left.at[k],
            flow_send_sem.at[last * blocks - k + 2 * lax.rem(k, blocks)],
            left_sem.at[k],
            device_id={"tp": lax.rem(z + 1, tp_count)},
            device_id_type=MESH,
        )

    def left_copy(k):
        return pltpu.make_async_remote_copy(
            stage.at[k],
            from_right.at[k],
            flow_send_sem.at[k],
            right_sem.at[k],
            device_id={"tp": lax.rem(z + last, tp_count)},
            device_id_type=MESH,
        )

    def base_part(chunk, block):
        part = jnp.dot(tok[chunk], weight[block], preferred_element_type=F32)
        return part.astype(BF16)

    def adapter_copy(which, hop):
        send, got = ((down_send, got_down), (up_send, got_up))[which]
        return pltpu.make_async_remote_copy(
            send.at[hop - 1],
            got.at[ad],
            adapter_send_sem.at[which, hop - 1],
            adapter_recv_sem.at[which, hop - 1],
            device_id={"ad": lax.rem(ad + hop, groups)},
            device_id_type=MESH,
        )

    def rank_copy(way):
        return pltpu.make_async_remote_copy(
            rank_send.at[way],
            rank_got.at[way],
            rank_send_sem.at[way],
            rank_recv_sem.at[way],
            device_id={"tp": lax.rem(z + (1 if way == 0 else last), tp_count)},
            device_id_type=MESH,
        )

    def places(group):
        found = []
        for q in range(requests):
            slot = slots_ref[ids_ref[group, q]]
            owner = jnp.int32(0)
            for g in range(1, groups):
                owner = owner + jnp.where(slot >= g * held, 1, 0)
            rank = jnp.int32(0)
            for earlier, _, _ in found:
                rank = rank + jnp.where(earlier == owner, 1, 0)
            found.append((owner, rank, slot - owner * held))
        return found

    def send_adapters():
        down_copy.wait()
        up_copy.wait()
        row = lax.broadcasted_iota(jnp.int32, (cap_rows, store_rows), 0)
        col = lax.broadcasted_iota(jnp.int32, (cap_rows, store_rows), 1)
        for hop in list(range(1, groups)) + [0]:
            wanted = jnp.full((cap_rows, store_rows), -1 - rank_extent, jnp.int32)
            for owner, rank, within in places(lax.rem(ad + hop, groups)):
                place = jnp.where(owner == ad, rank, -1)
                wanted = jnp.where((row >> rank_bits) == place, within * rank_extent, wanted)
            chosen = one_hot(col == wanted + (row & (rank_extent - 1)))
            for which, (store, send, got) in enumerate(
                ((down, down_send, got_down), (up, up_send, got_up))
            ):
                picked = jnp.dot(chosen, store[...], preferred_element_type=F32).astype(BF16)
                if hop > 0:
                    send[hop - 1] = picked
                    adapter_copy(which, hop).start()
                else:
                    got[ad] = picked

    def token_mask(first, count):
        lane = lax.broadcasted_iota(jnp.int32, (1, lanes), 1) >> rank_bits
        starts = jnp.zeros((1, lanes), jnp.int32)
        ends = jnp.zeros((1, lanes), jnp.int32)
        position = jnp.int32(0)
        for q, (owner, rank, _) in enumerate(places(ad)):
            here = lane == owner * CAP + rank
            starts = jnp.where(here, position, starts)
            position = position + lengths_ref[0, q]
            ends = jnp.where(here, position, ends)
        at = first + lax.broadcasted_iota(jnp.int32, (count, lanes), 0)
        return (at >= starts) & (at < ends)

    def rank_hot():
        lane = lax.broadcasted_iota(jnp.int32, (rank_extent, lanes), 1)
        row = lax.broadcasted_iota(jnp.int32, (rank_extent, lanes), 0)
        return one_hot((lane & (rank_extent - 1)) == row)

    def send_ranks():
        for hop in range(1, groups):
            adapter_copy(0, hop).wait()
        acts = lax.dot_general(
            tok[...].reshape(tp_count * rows, -1),
            got_down[...].reshape(lanes, -1),
            (((1,), (1,)), ((), ())),
            preferred_element_type=F32,
        )
        acts = jnp.where(token_mask(0, tp_count * rows), acts, 0.0).astype(BF16)
        for chunk in range(tp_count):
            rank_own[chunk] = lax.dot_general(
                rank_hot(),
                acts[chunk * rows : (chunk + 1) * rows],
                (((1,), (1,)), ((), ())),
                preferred_element_type=F32,
            ).astype(BF16)

    def pass_ranks(way):
        @pl.when(z == (0 if way == 0 else last))
        def _():
            rank_send[way] = rank_own[...]

        @pl.when(z != (0 if way == 0 else last))
        def _():
            rank_copy(way).wait_recv()
            rank_send[way] = (rank_own[...].astype(F32) + rank_got[way].astype(F32)).astype(BF16)

        rank_copy(way).start()

    def expand_ranks():
        for hop in range(1, groups):
            adapter_copy(1, hop).wait()
        rank_sum[...] = rank_own[z].astype(F32)

        @pl.when(z == last)
        def _():
            rank_copy(0).wait_recv()

        @pl.when(z > 0)
        def _():
            rank_sum[...] += rank_got[0, z].astype(F32)

        @pl.when(z == 0)
        def _():
            rank_copy(1).wait_recv()

        @pl.when(z < last)
        def _():
            rank_sum[...] += rank_got[1, z].astype(F32)

        spread = lax.dot_general(
            rank_sum[...].astype(BF16),
            rank_hot(),
            (((0,), (0,)), ((), ())),
            preferred_element_type=F32,
        )
        expanded[...] = jnp.where(token_mask(z * rows, rows), spread, 0.0).astype(BF16)

    right_count = (last - z) * blocks
    left_count = z * blocks
    final_step = (tp_count - 2) * blocks + LAG

    rank_step = blocks + 1

    tok_copy(first).wait()
    weight_copy(0).wait()

    @pl.when((z == 0) | (z == last))
    def _():
        stage[first * blocks] = base_part(first, 0)

    neighbours = jnp.where(z > 0, 1, 0) + jnp.where(z < last, 1, 0)
    pl.semaphore_wait(barrier, neighbours + groups - 1)

    def step(s, carry):
        @pl.when((s > 0) & (s < blocks))
        def _():
            weight_copy(s).wait()

        @pl.when(s == 1)
        def _():
            tok_copy(last - first).wait()
            for chunk in range(1, last):
                tok_copy(chunk).wait()

        k_right = s - LAG * z

        @pl.when((k_right >= DEPTH) & (k_right < right_count + DEPTH))
        def _():
            right_copy(k_right - DEPTH).wait_send()

        @pl.when((k_right >= 0) & (k_right < right_count))
        def _():
            chunk = last - k_right // blocks
            block = lax.rem(k_right, blocks)
            at = chunk * blocks + block

            @pl.when((z == 0) & (s > 0))
            def _():
                stage[at] = base_part(chunk, block)

            @pl.when(z > 0)
            def _():
                part = base_part(chunk, block)
                right_copy(k_right).wait_recv()
                stage[at] = (part.astype(F32) + from_left[k_right].astype(F32)).astype(BF16)

            right_copy(k_right).start()

        k_left = s - LAG * (last - z)

        @pl.when((k_left >= DEPTH) & (k_left < left_count + DEPTH))
        def _():
            left_copy(k_left - DEPTH).wait_send()

        @pl.when((k_left >= 0) & (k_left < left_count))
        def _():
            chunk = k_left // blocks
            block = lax.rem(k_left, blocks)

            @pl.when((z == last) & (s > 0))
            def _():
                stage[k_left] = base_part(chunk, block)

            @pl.when(z < last)
            def _():
                part = base_part(chunk, block)
                left_copy(k_left).wait_recv()
                stage[k_left] = (part.astype(F32) + from_right[k_left].astype(F32)).astype(BF16)

            left_copy(k_left).start()

        @pl.when(s == 1)
        def _():
            send_adapters()

        @pl.when(s == rank_step)
        def _():
            send_ranks()

        @pl.when((s == rank_step + z) & (z < last))
        def _():
            pass_ranks(0)

        @pl.when((s == rank_step + last - z) & (z > 0))
        def _():
            pass_ranks(1)

        @pl.when(s == final_step - 1)
        def _():
            expand_ranks()

        block = s - final_step

        @pl.when((block >= 0) & (block < blocks))
        def _():
            cols = pl.ds(pl.multiple_of(block * BLOCK_COLS, BLOCK_COLS), BLOCK_COLS)
            lora = jnp.dot(
                expanded[...],
                got_up[:, :, cols].reshape(lanes, BLOCK_COLS),
                preferred_element_type=F32,
            )
            total[...] = base_part(z, block).astype(F32) + ADAPTER_SCALE * lora

            @pl.when(z < last)
            def _():
                left_copy(left_count + block).wait_recv()
                total[...] += from_right[left_count + block].astype(F32)

            @pl.when(z > 0)
            def _():
                right_copy(right_count + block).wait_recv()
                total[...] += from_left[right_count + block].astype(F32)

            out[:, cols] = total[...].astype(BF16)

        return carry

    lax.fori_loop(0, last * blocks + max(LAG, DEPTH), step, 0)

    @pl.when(z < last)
    def _():
        rank_copy(0).wait_send()

    @pl.when(z > 0)
    def _():
        rank_copy(1).wait_send()


def local(
    tokens,
    query_weight_matrix,
    adapter_down_weight,
    adapter_up_weight,
    request_adapter_id,
    request_token_length,
    adapter_store_slot,
):
    tp_count = lax.axis_size("tp")
    groups = lax.axis_size("ad")
    tok_rows, width = tokens.shape[1:]
    cols = query_weight_matrix.shape[1]
    held, rank_extent = adapter_down_weight.shape[:2]
    rows = tok_rows // tp_count
    blocks = cols // BLOCK_COLS
    cap_rows = CAP * rank_extent
    block = (rows, BLOCK_COLS)
    flow = (tp_count - 1) * blocks
    hbm = pl.BlockSpec(memory_space=pltpu.HBM)
    smem = pl.BlockSpec(memory_space=pltpu.SMEM)
    dma = pltpu.SemaphoreType.DMA
    query = pl.pallas_call(
        functools.partial(kernel, tp_count, groups, rank_extent),
        out_shape=pltpu.VMEM((rows, cols), BF16),
        in_specs=[hbm] * 4 + [smem] * 3,
        out_specs=pl.BlockSpec(memory_space=pltpu.VMEM),
        scratch_shapes=[
            pltpu.VMEM((tp_count, rows, width), BF16),
            pltpu.VMEM((blocks, width, BLOCK_COLS), BF16),
            pltpu.VMEM((held * rank_extent, width), BF16),
            pltpu.VMEM((held * rank_extent, cols), BF16),
            pltpu.VMEM((tp_count * blocks, *block), BF16),
            pltpu.VMEM((flow, *block), BF16),
            pltpu.VMEM((flow, *block), BF16),
            pltpu.VMEM((groups - 1, cap_rows, width), BF16),
            pltpu.VMEM((groups - 1, cap_rows, cols), BF16),
            pltpu.VMEM((groups, cap_rows, width), BF16),
            pltpu.VMEM((groups, cap_rows, cols), BF16),
            pltpu.VMEM((tp_count, rank_extent, rows), BF16),
            pltpu.VMEM((2, tp_count, rank_extent, rows), BF16),
            pltpu.VMEM((2, tp_count, rank_extent, rows), BF16),
            pltpu.VMEM((rank_extent, rows), F32),
            pltpu.VMEM((rows, groups * cap_rows), BF16),
            pltpu.VMEM(block, F32),
            dma((tp_count,)),
            dma((blocks,)),
            dma((2,)),
            dma((tp_count * blocks,)),
            dma((flow,)),
            dma((flow,)),
            dma((2, groups - 1)),
            dma((2, groups - 1)),
            dma((2,)),
            dma((2,)),
        ],
        compiler_params=pltpu.CompilerParams(
            collective_id=0, has_side_effects=True, vmem_limit_bytes=56 * 2**20
        ),
        cost_estimate=pl.CostEstimate(
            flops=2 * tok_rows * width * cols,
            bytes_accessed=2 * width * (cols + tok_rows),
            transcendentals=0,
        ),
        name="query_projection",
    )(
        tokens.reshape(tok_rows, width),
        query_weight_matrix,
        adapter_down_weight.reshape(held * rank_extent, width),
        adapter_up_weight.reshape(held * rank_extent, cols),
        request_adapter_id,
        request_token_length,
        adapter_store_slot,
    )
    return query[None]


def solution(mesh):
    return jax.shard_map(
        local,
        mesh=mesh,
        in_specs=(
            P(("rep", "ad"), None, "tp"),
            P("tp", "sub"),
            P("ad", None, "tp"),
            P("ad", None, "sub"),
            P("rep", None),
            P(("rep", "ad"), None),
            P("rep"),
        ),
        out_specs=P(("rep", "ad"), "tp", "sub"),
        check_vma=False,
    )
```

```python
import functools
import jax
import jax.numpy as jnp
from jax import lax
from jax.experimental import pallas as pl
from jax.experimental.pallas import tpu as pltpu
from jax.sharding import PartitionSpec as P

CAP = 4

ADAPTER_SCALE = 2.0

BLOCK_COLS = 512
PIECES = ((0, 128), (128, 384))
LAG = 2
DEPTH = 4

MESH = pl.DeviceIdType.MESH
F32 = jnp.float32
BF16 = jnp.bfloat16


def one_hot(condition):
    return jnp.where(condition, 1.0, 0.0).astype(BF16)


def kernel(
    tp_count,
    groups,
    rank_extent,
    tokens_hbm,
    weight_hbm,
    down_hbm,
    up_hbm,
    ids_hbm,
    lengths_hbm,
    slots_hbm,
    out,
    tok,
    weight,
    down,
    up,
    stage,
    from_left,
    from_right,
    down_send,
    up_send,
    got_down,
    got_up,
    rank_own,
    rank_send,
    rank_got,
    rank_sum,
    total,
    ids_ref,
    lengths_ref,
    slots_ref,
    tok_sem,
    weight_sem,
    store_sem,
    small_sem,
    flow_send_sem,
    left_sem,
    right_sem,
    adapter_send_sem,
    adapter_recv_sem,
    rank_send_sem,
    rank_recv_sem,
    piece_weight_sem,
    piece_send_sem,
    piece_recv_sem,
):
    z = lax.axis_index("tp")
    ad = lax.axis_index("ad")
    rows = tok.shape[1]
    blocks = weight.shape[0]
    requests = ids_ref.shape[1]
    store_rows = down.shape[0]
    held = store_rows // rank_extent
    cap_rows = CAP * rank_extent
    lanes = groups * cap_rows
    rank_bits = rank_extent.bit_length() - 1
    last = tp_count - 1

    def tok_copy(chunk):
        return pltpu.make_async_copy(
            tokens_hbm.at[pl.ds(chunk * rows, rows), :], tok.at[chunk], tok_sem.at[chunk]
        )

    def weight_copy(block):
        return pltpu.make_async_copy(
            weight_hbm.at[:, pl.ds(pl.multiple_of(block * BLOCK_COLS, BLOCK_COLS), BLOCK_COLS)],
            weight.at[block],
            weight_sem.at[block],
        )

    def first_weight_copy(i):
        cols = pl.ds(*PIECES[i])
        return pltpu.make_async_copy(
            weight_hbm.at[:, cols], weight.at[0, :, cols], piece_weight_sem.at[i]
        )

    down_copy = pltpu.make_async_copy(down_hbm, down, store_sem.at[0])
    up_copy = pltpu.make_async_copy(up_hbm, up, store_sem.at[1])
    small_copies = [
        pltpu.make_async_copy(source, target, small_sem.at[i])
        for i, (source, target) in enumerate(
            ((ids_hbm, ids_ref), (lengths_hbm, lengths_ref), (slots_hbm, slots_ref))
        )
    ]
    barrier = pltpu.get_barrier_semaphore()

    def greet(target):
        pl.semaphore_signal(barrier, inc=1, device_id=target, device_id_type=MESH)

    @pl.when(z < last)
    def _():
        greet({"tp": lax.rem(z + 1, tp_count)})

    @pl.when(z > 0)
    def _():
        greet({"tp": lax.rem(z + last, tp_count)})

    for hop in range(1, groups):
        greet({"ad": lax.rem(ad + hop, groups)})

    first = jnp.where(z == last, 0, last)
    first_weight_copy(0).start()
    tok_copy(first).start()
    for i in range(1, len(PIECES)):
        first_weight_copy(i).start()
    weight_copy(1).start()
    tok_copy(last - first).start()
    for chunk in range(1, last):
        tok_copy(chunk).start()
    for small in small_copies:
        small.start()
    down_copy.start()
    up_copy.start()
    for block in range(2, blocks):
        weight_copy(block).start()

    def right_copy(k):
        return pltpu.make_async_remote_copy(
            stage.at[last * blocks - k + 2 * lax.rem(k, blocks)],
            from_left.at[k],
            flow_send_sem.at[last * blocks - k + 2 * lax.rem(k, blocks)],
            left_sem.at[k],
            device_id={"tp": lax.rem(z + 1, tp_count)},
            device_id_type=MESH,
        )

    def left_copy(k):
        return pltpu.make_async_remote_copy(
            stage.at[k],
            from_right.at[k],
            flow_send_sem.at[k],
            right_sem.at[k],
            device_id={"tp": lax.rem(z + last, tp_count)},
            device_id_type=MESH,
        )

    def piece_copy(way, i):
        cols = pl.ds(*PIECES[i])
        got, at, hop = ((from_left, last * blocks, 1), (from_right, 0, last))[way]
        return pltpu.make_async_remote_copy(
            stage.at[at, :, cols],
            got.at[0, :, cols],
            piece_send_sem.at[way, i],
            piece_recv_sem.at[way, i],
            device_id={"tp": lax.rem(z + hop, tp_count)},
            device_id_type=MESH,
        )

    def base_part(chunk, block):
        part = jnp.dot(tok[chunk], weight[block], preferred_element_type=F32)
        return part.astype(BF16)

    def adapter_copy(which, hop):
        send, got = ((down_send, got_down), (up_send, got_up))[which]
        return pltpu.make_async_remote_copy(
            send.at[hop - 1],
            got.at[ad],
            adapter_send_sem.at[which, hop - 1],
            adapter_recv_sem.at[which, hop - 1],
            device_id={"ad": lax.rem(ad + hop, groups)},
            device_id_type=MESH,
        )

    def rank_copy(way):
        return pltpu.make_async_remote_copy(
            rank_send.at[way],
            rank_got.at[way],
            rank_send_sem.at[way],
            rank_recv_sem.at[way],
            device_id={"tp": lax.rem(z + (1 if way == 0 else last), tp_count)},
            device_id_type=MESH,
        )

    def places(group):
        found = []
        for q in range(requests):
            slot = slots_ref[ids_ref[group, q]]
            owner = jnp.int32(0)
            for g in range(1, groups):
                owner = owner + jnp.where(slot >= g * held, 1, 0)
            rank = jnp.int32(0)
            for earlier, _, _ in found:
                rank = rank + jnp.where(earlier == owner, 1, 0)
            found.append((owner, rank, slot - owner * held))
        return found

    def send_adapters():
        for small in small_copies:
            small.wait()
        down_copy.wait()
        up_copy.wait()
        row = lax.broadcasted_iota(jnp.int32, (cap_rows, store_rows), 0)
        col = lax.broadcasted_iota(jnp.int32, (cap_rows, store_rows), 1)
        for hop in list(range(1, groups)) + [0]:
            wanted = jnp.full((cap_rows, store_rows), -1 - rank_extent, jnp.int32)
            for owner, rank, within in places(lax.rem(ad + hop, groups)):
                place = jnp.where(owner == ad, rank, -1)
                wanted = jnp.where((row >> rank_bits) == place, within * rank_extent, wanted)
            chosen = one_hot(col == wanted + (row & (rank_extent - 1)))
            for which, (store, send, got) in enumerate(
                ((down, down_send, got_down), (up, up_send, got_up))
            ):
                picked = jnp.dot(chosen, store[...], preferred_element_type=F32).astype(BF16)
                if hop > 0:
                    send[hop - 1] = picked
                    adapter_copy(which, hop).start()
                else:
                    got[ad] = picked

    def token_mask(first, count):
        lane = lax.broadcasted_iota(jnp.int32, (1, lanes), 1) >> rank_bits
        starts = jnp.zeros((1, lanes), jnp.int32)
        ends = jnp.zeros((1, lanes), jnp.int32)
        position = jnp.int32(0)
        for q, (owner, rank, _) in enumerate(places(ad)):
            here = lane == owner * CAP + rank
            starts = jnp.where(here, position, starts)
            position = position + lengths_ref[0, q]
            ends = jnp.where(here, position, ends)
        at = first + lax.broadcasted_iota(jnp.int32, (count, lanes), 0)
        return (at >= starts) & (at < ends)

    def rank_hot():
        lane = lax.broadcasted_iota(jnp.int32, (rank_extent, lanes), 1)
        row = lax.broadcasted_iota(jnp.int32, (rank_extent, lanes), 0)
        return one_hot((lane & (rank_extent - 1)) == row)

    def send_ranks():
        for hop in range(1, groups):
            adapter_copy(0, hop).wait()
        acts = lax.dot_general(
            tok[...].reshape(tp_count * rows, -1),
            got_down[...].reshape(lanes, -1),
            (((1,), (1,)), ((), ())),
            preferred_element_type=F32,
        )
        acts = jnp.where(token_mask(0, tp_count * rows), acts, 0.0).astype(BF16)
        for chunk in range(tp_count):
            rank_own[chunk] = lax.dot_general(
                rank_hot(),
                acts[chunk * rows : (chunk + 1) * rows],
                (((1,), (1,)), ((), ())),
                preferred_element_type=F32,
            ).astype(BF16)

    def pass_ranks(way):
        @pl.when(z == (0 if way == 0 else last))
        def _():
            rank_send[way] = rank_own[...]

        @pl.when(z != (0 if way == 0 else last))
        def _():
            rank_copy(way).wait_recv()
            rank_send[way] = (rank_own[...].astype(F32) + rank_got[way].astype(F32)).astype(BF16)

        rank_copy(way).start()

    def expand_ranks():
        for hop in range(1, groups):
            adapter_copy(1, hop).wait()
        rank_sum[...] = rank_own[z].astype(F32)

        @pl.when(z == last)
        def _():
            rank_copy(0).wait_recv()

        @pl.when(z > 0)
        def _():
            rank_sum[...] += rank_got[0, z].astype(F32)

        @pl.when(z == 0)
        def _():
            rank_copy(1).wait_recv()

        @pl.when(z < last)
        def _():
            rank_sum[...] += rank_got[1, z].astype(F32)

        spread = lax.dot_general(
            rank_sum[...].astype(BF16),
            rank_hot(),
            (((0,), (0,)), ((), ())),
            preferred_element_type=F32,
        )
        expanded = jnp.where(token_mask(z * rows, rows), spread, 0.0).astype(BF16)

        def own(block, carry):
            cols = pl.ds(pl.multiple_of(block * BLOCK_COLS, BLOCK_COLS), BLOCK_COLS)
            lora = jnp.dot(
                expanded,
                got_up[:, :, cols].reshape(lanes, BLOCK_COLS),
                preferred_element_type=F32,
            )
            total[block] = base_part(z, block).astype(F32) + ADAPTER_SCALE * lora
            return carry

        lax.fori_loop(0, blocks, own, 0)

    right_count = (last - z) * blocks
    left_count = z * blocks
    final_step = (tp_count - 2) * blocks + LAG

    rank_step = blocks + 1

    neighbours = jnp.where(z > 0, 1, 0) + jnp.where(z < last, 1, 0)
    tok_copy(first).wait()
    for i, (low, count) in enumerate(PIECES):
        cols = pl.ds(low, count)
        first_weight_copy(i).wait()

        @pl.when((z == 0) | (z == last))
        def _():
            part = jnp.dot(tok[first], weight[0, :, cols], preferred_element_type=F32)
            stage[first * blocks, :, cols] = part.astype(BF16)

        if i == 0:
            pl.semaphore_wait(barrier, neighbours + groups - 1)

        for way, end in enumerate((0, last)):

            @pl.when(z == end)
            def _():
                piece_copy(way, i).start()

    def step(s, carry):
        @pl.when((s > 0) & (s < blocks))
        def _():
            weight_copy(s).wait()

        @pl.when(s == 1)
        def _():
            tok_copy(last - first).wait()
            for chunk in range(1, last):
                tok_copy(chunk).wait()

        k_right = s - LAG * z

        @pl.when((k_right >= DEPTH) & (k_right < right_count + DEPTH))
        def _():
            @pl.when((z == 0) & (k_right == DEPTH))
            def _():
                for i in range(len(PIECES)):
                    piece_copy(0, i).wait_send()

            @pl.when((z != 0) | (k_right > DEPTH))
            def _():
                right_copy(k_right - DEPTH).wait_send()

        @pl.when((k_right >= 0) & (k_right < right_count))
        def _():
            chunk = last - k_right // blocks
            block = lax.rem(k_right, blocks)
            at = chunk * blocks + block

            @pl.when((z == 0) & (s > 0))
            def _():
                stage[at] = base_part(chunk, block)

            @pl.when(z > 0)
            def _():
                part = base_part(chunk, block)

                @pl.when((z == 1) & (k_right == 0))
                def _():
                    for i in range(len(PIECES)):
                        piece_copy(0, i).wait_recv()

                @pl.when((z != 1) | (k_right > 0))
                def _():
                    right_copy(k_right).wait_recv()

                stage[at] = (part.astype(F32) + from_left[k_right].astype(F32)).astype(BF16)

            @pl.when((z != 0) | (s > 0))
            def _():
                right_copy(k_right).start()

        k_left = s - LAG * (last - z)

        @pl.when((k_left >= DEPTH) & (k_left < left_count + DEPTH))
        def _():
            @pl.when((z == last) & (k_left == DEPTH))
            def _():
                for i in range(len(PIECES)):
                    piece_copy(1, i).wait_send()

            @pl.when((z != last) | (k_left > DEPTH))
            def _():
                left_copy(k_left - DEPTH).wait_send()

        @pl.when((k_left >= 0) & (k_left < left_count))
        def _():
            chunk = k_left // blocks
            block = lax.rem(k_left, blocks)

            @pl.when((z == last) & (s > 0))
            def _():
                stage[k_left] = base_part(chunk, block)

            @pl.when(z < last)
            def _():
                part = base_part(chunk, block)

                @pl.when((z == last - 1) & (k_left == 0))
                def _():
                    for i in range(len(PIECES)):
                        piece_copy(1, i).wait_recv()

                @pl.when((z != last - 1) | (k_left > 0))
                def _():
                    left_copy(k_left).wait_recv()

                stage[k_left] = (part.astype(F32) + from_right[k_left].astype(F32)).astype(BF16)

            @pl.when((z != last) | (s > 0))
            def _():
                left_copy(k_left).start()

        @pl.when(s == 1)
        def _():
            send_adapters()

        @pl.when(s == rank_step)
        def _():
            send_ranks()

        @pl.when((s == rank_step + z) & (z < last))
        def _():
            pass_ranks(0)

        @pl.when((s == rank_step + last - z) & (z > 0))
        def _():
            pass_ranks(1)

        @pl.when(s == final_step - 1)
        def _():
            expand_ranks()

        block = s - final_step

        @pl.when((block >= 0) & (block < blocks))
        def _():
            cols = pl.ds(pl.multiple_of(block * BLOCK_COLS, BLOCK_COLS), BLOCK_COLS)

            @pl.when(z < last)
            def _():
                left_copy(left_count + block).wait_recv()
                total[block] += from_right[left_count + block].astype(F32)

            @pl.when(z > 0)
            def _():
                right_copy(right_count + block).wait_recv()
                total[block] += from_left[right_count + block].astype(F32)

            out[:, cols] = total[block].astype(BF16)

        return carry

    lax.fori_loop(0, last * blocks + max(LAG, DEPTH), step, 0)

    @pl.when(z < last)
    def _():
        rank_copy(0).wait_send()

    @pl.when(z > 0)
    def _():
        rank_copy(1).wait_send()


def local(
    tokens,
    query_weight_matrix,
    adapter_down_weight,
    adapter_up_weight,
    request_adapter_id,
    request_token_length,
    adapter_store_slot,
):
    tp_count = lax.axis_size("tp")
    groups = lax.axis_size("ad")
    tok_rows, width = tokens.shape[1:]
    cols = query_weight_matrix.shape[1]
    held, rank_extent = adapter_down_weight.shape[:2]
    rows = tok_rows // tp_count
    blocks = cols // BLOCK_COLS
    cap_rows = CAP * rank_extent
    block = (rows, BLOCK_COLS)
    flow = (tp_count - 1) * blocks
    hbm = pl.BlockSpec(memory_space=pltpu.HBM)
    dma = pltpu.SemaphoreType.DMA
    query = pl.pallas_call(
        functools.partial(kernel, tp_count, groups, rank_extent),
        out_shape=pltpu.VMEM((rows, cols), BF16),
        in_specs=[hbm] * 7,
        out_specs=pl.BlockSpec(memory_space=pltpu.VMEM),
        scratch_shapes=[
            pltpu.VMEM((tp_count, rows, width), BF16),
            pltpu.VMEM((blocks, width, BLOCK_COLS), BF16),
            pltpu.VMEM((held * rank_extent, width), BF16),
            pltpu.VMEM((held * rank_extent, cols), BF16),
            pltpu.VMEM((tp_count * blocks, *block), BF16),
            pltpu.VMEM((flow, *block), BF16),
            pltpu.VMEM((flow, *block), BF16),
            pltpu.VMEM((groups - 1, cap_rows, width), BF16),
            pltpu.VMEM((groups - 1, cap_rows, cols), BF16),
            pltpu.VMEM((groups, cap_rows, width), BF16),
            pltpu.VMEM((groups, cap_rows, cols), BF16),
            pltpu.VMEM((tp_count, rank_extent, rows), BF16),
            pltpu.VMEM((2, tp_count, rank_extent, rows), BF16),
            pltpu.VMEM((2, tp_count, rank_extent, rows), BF16),
            pltpu.VMEM((rank_extent, rows), F32),
            pltpu.VMEM((blocks, *block), F32),
            pltpu.SMEM(request_adapter_id.shape, jnp.int32),
            pltpu.SMEM(request_token_length.shape, jnp.int32),
            pltpu.SMEM(adapter_store_slot.shape, jnp.int32),
            dma((tp_count,)),
            dma((blocks,)),
            dma((2,)),
            dma((3,)),
            dma((tp_count * blocks,)),
            dma((flow,)),
            dma((flow,)),
            dma((2, groups - 1)),
            dma((2, groups - 1)),
            dma((2,)),
            dma((2,)),
            dma((len(PIECES),)),
            dma((2, len(PIECES))),
            dma((2, len(PIECES))),
        ],
        compiler_params=pltpu.CompilerParams(
            collective_id=0, has_side_effects=True, vmem_limit_bytes=56 * 2**20
        ),
        cost_estimate=pl.CostEstimate(
            flops=2 * tok_rows * width * cols,
            bytes_accessed=2 * width * (cols + tok_rows),
            transcendentals=0,
        ),
        name="query_projection",
    )(
        tokens.reshape(tok_rows, width),
        query_weight_matrix,
        adapter_down_weight.reshape(held * rank_extent, width),
        adapter_up_weight.reshape(held * rank_extent, cols),
        request_adapter_id,
        request_token_length,
        adapter_store_slot,
    )
    return query[None]


def solution(mesh):
    return jax.shard_map(
        local,
        mesh=mesh,
        in_specs=(
            P(("rep", "ad"), None, "tp"),
            P("tp", "sub"),
            P("ad", None, "tp"),
            P("ad", None, "sub"),
            P("rep", None),
            P(("rep", "ad"), None),
            P("rep"),
        ),
        out_specs=P(("rep", "ad"), "tp", "sub"),
        check_vma=False,
    )
```

```python
import functools
import jax
import jax.numpy as jnp
from jax import lax
from jax.experimental import pallas as pl
from jax.experimental.pallas import tpu as pltpu
from jax.sharding import PartitionSpec as P

CAP = 4

ADAPTER_SCALE = 2.0

BLOCK_COLS = 512
PIECES = ((0, 128), (128, 128), (256, 256))
LAG = 3
DEPTH = 2

MESH = pl.DeviceIdType.MESH
F32 = jnp.float32
BF16 = jnp.bfloat16


def one_hot(condition):
    return jnp.where(condition, 1.0, 0.0).astype(BF16)


def kernel(
    tp_count,
    groups,
    rank_extent,
    tokens_hbm,
    weight_hbm,
    down_hbm,
    up_hbm,
    ids_hbm,
    lengths_hbm,
    slots_hbm,
    out,
    tok,
    weight,
    down,
    up,
    stage,
    from_left,
    from_right,
    down_send,
    up_send,
    got_down,
    got_up,
    rank_own,
    rank_send,
    rank_got,
    rank_sum,
    total,
    ids_ref,
    lengths_ref,
    slots_ref,
    tok_sem,
    weight_sem,
    store_sem,
    small_sem,
    flow_send_sem,
    left_sem,
    right_sem,
    adapter_send_sem,
    adapter_recv_sem,
    rank_send_sem,
    rank_recv_sem,
    piece_weight_sem,
    piece_send_sem,
    piece_recv_sem,
):
    z = lax.axis_index("tp")
    ad = lax.axis_index("ad")
    rows = tok.shape[1]
    blocks = weight.shape[0]
    requests = ids_ref.shape[1]
    store_rows = down.shape[0]
    held = store_rows // rank_extent
    cap_rows = CAP * rank_extent
    lanes = groups * cap_rows
    rank_bits = rank_extent.bit_length() - 1
    last = tp_count - 1

    def tok_copy(chunk):
        return pltpu.make_async_copy(
            tokens_hbm.at[pl.ds(chunk * rows, rows), :], tok.at[chunk], tok_sem.at[chunk]
        )

    def weight_copy(block):
        return pltpu.make_async_copy(
            weight_hbm.at[:, pl.ds(pl.multiple_of(block * BLOCK_COLS, BLOCK_COLS), BLOCK_COLS)],
            weight.at[block],
            weight_sem.at[block],
        )

    def first_weight_copy(i):
        cols = pl.ds(*PIECES[i])
        return pltpu.make_async_copy(
            weight_hbm.at[:, cols], weight.at[0, :, cols], piece_weight_sem.at[i]
        )

    down_copy = pltpu.make_async_copy(down_hbm, down, store_sem.at[0])
    up_copy = pltpu.make_async_copy(up_hbm, up, store_sem.at[1])
    small_copies = [
        pltpu.make_async_copy(source, target, small_sem.at[i])
        for i, (source, target) in enumerate(
            ((ids_hbm, ids_ref), (lengths_hbm, lengths_ref), (slots_hbm, slots_ref))
        )
    ]
    first = jnp.where(z == last, 0, last)
    first_weight_copy(0).start()
    tok_copy(first).start()

    barrier = pltpu.get_barrier_semaphore()

    def greet(target):
        pl.semaphore_signal(barrier, inc=1, device_id=target, device_id_type=MESH)

    @pl.when(z < last)
    def _():
        greet({"tp": lax.rem(z + 1, tp_count)})

    @pl.when(z > 0)
    def _():
        greet({"tp": lax.rem(z + last, tp_count)})

    for hop in range(1, groups):
        greet({"ad": lax.rem(ad + hop, groups)})

    for i in range(1, len(PIECES)):
        first_weight_copy(i).start()
    weight_copy(1).start()
    tok_copy(last - first).start()
    for chunk in range(1, last):
        tok_copy(chunk).start()
    for small in small_copies:
        small.start()
    down_copy.start()
    up_copy.start()
    for block in range(2, blocks):
        weight_copy(block).start()

    def right_copy(k):
        return pltpu.make_async_remote_copy(
            stage.at[last * blocks - k + 2 * lax.rem(k, blocks)],
            from_left.at[k],
            flow_send_sem.at[last * blocks - k + 2 * lax.rem(k, blocks)],
            left_sem.at[k],
            device_id={"tp": lax.rem(z + 1, tp_count)},
            device_id_type=MESH,
        )

    def left_copy(k):
        return pltpu.make_async_remote_copy(
            stage.at[k],
            from_right.at[k],
            flow_send_sem.at[k],
            right_sem.at[k],
            device_id={"tp": lax.rem(z + last, tp_count)},
            device_id_type=MESH,
        )

    def piece_copy(way, i):
        cols = pl.ds(*PIECES[i])
        got, at, hop = ((from_left, last * blocks, 1), (from_right, 0, last))[way]
        return pltpu.make_async_remote_copy(
            stage.at[at, :, cols],
            got.at[0, :, cols],
            piece_send_sem.at[way, i],
            piece_recv_sem.at[way, i],
            device_id={"tp": lax.rem(z + hop, tp_count)},
            device_id_type=MESH,
        )

    def base_part(chunk, block):
        part = jnp.dot(tok[chunk], weight[block], preferred_element_type=F32)
        return part.astype(BF16)

    def adapter_copy(which, hop):
        send, got = ((down_send, got_down), (up_send, got_up))[which]
        return pltpu.make_async_remote_copy(
            send.at[hop - 1],
            got.at[ad],
            adapter_send_sem.at[which, hop - 1],
            adapter_recv_sem.at[which, hop - 1],
            device_id={"ad": lax.rem(ad + hop, groups)},
            device_id_type=MESH,
        )

    def rank_copy(way):
        return pltpu.make_async_remote_copy(
            rank_send.at[way],
            rank_got.at[way],
            rank_send_sem.at[way],
            rank_recv_sem.at[way],
            device_id={"tp": lax.rem(z + (1 if way == 0 else last), tp_count)},
            device_id_type=MESH,
        )

    def places(group):
        found = []
        for q in range(requests):
            slot = slots_ref[ids_ref[group, q]]
            owner = jnp.int32(0)
            for g in range(1, groups):
                owner = owner + jnp.where(slot >= g * held, 1, 0)
            rank = jnp.int32(0)
            for earlier, _, _ in found:
                rank = rank + jnp.where(earlier == owner, 1, 0)
            found.append((owner, rank, slot - owner * held))
        return found

    def send_adapters():
        for small in small_copies:
            small.wait()
        down_copy.wait()
        up_copy.wait()
        row = lax.broadcasted_iota(jnp.int32, (cap_rows, store_rows), 0)
        col = lax.broadcasted_iota(jnp.int32, (cap_rows, store_rows), 1)
        for hop in list(range(1, groups)) + [0]:
            wanted = jnp.full((cap_rows, store_rows), -1 - rank_extent, jnp.int32)
            for owner, rank, within in places(lax.rem(ad + hop, groups)):
                place = jnp.where(owner == ad, rank, -1)
                wanted = jnp.where((row >> rank_bits) == place, within * rank_extent, wanted)
            chosen = one_hot(col == wanted + (row & (rank_extent - 1)))
            for which, (store, send, got) in enumerate(
                ((down, down_send, got_down), (up, up_send, got_up))
            ):
                picked = jnp.dot(chosen, store[...], preferred_element_type=F32).astype(BF16)
                if hop > 0:
                    send[hop - 1] = picked
                    adapter_copy(which, hop).start()
                else:
                    got[ad] = picked

    def token_mask(first, count):
        lane = lax.broadcasted_iota(jnp.int32, (1, lanes), 1) >> rank_bits
        starts = jnp.zeros((1, lanes), jnp.int32)
        ends = jnp.zeros((1, lanes), jnp.int32)
        position = jnp.int32(0)
        for q, (owner, rank, _) in enumerate(places(ad)):
            here = lane == owner * CAP + rank
            starts = jnp.where(here, position, starts)
            position = position + lengths_ref[0, q]
            ends = jnp.where(here, position, ends)
        at = first + lax.broadcasted_iota(jnp.int32, (count, lanes), 0)
        return (at >= starts) & (at < ends)

    def rank_hot():
        lane = lax.broadcasted_iota(jnp.int32, (rank_extent, lanes), 1)
        row = lax.broadcasted_iota(jnp.int32, (rank_extent, lanes), 0)
        return one_hot((lane & (rank_extent - 1)) == row)

    def send_ranks():
        for hop in range(1, groups):
            adapter_copy(0, hop).wait()
        acts = lax.dot_general(
            tok[...].reshape(tp_count * rows, -1),
            got_down[...].reshape(lanes, -1),
            (((1,), (1,)), ((), ())),
            preferred_element_type=F32,
        )
        acts = jnp.where(token_mask(0, tp_count * rows), acts, 0.0).astype(BF16)
        for chunk in range(tp_count):
            rank_own[chunk] = lax.dot_general(
                rank_hot(),
                acts[chunk * rows : (chunk + 1) * rows],
                (((1,), (1,)), ((), ())),
                preferred_element_type=F32,
            ).astype(BF16)

    def pass_ranks(way):
        @pl.when(z == (0 if way == 0 else last))
        def _():
            rank_send[way] = rank_own[...]

        @pl.when(z != (0 if way == 0 else last))
        def _():
            rank_copy(way).wait_recv()
            rank_send[way] = (rank_own[...].astype(F32) + rank_got[way].astype(F32)).astype(BF16)

        rank_copy(way).start()

    def expand_ranks():
        for hop in range(1, groups):
            adapter_copy(1, hop).wait()
        rank_sum[...] = rank_own[z].astype(F32)

        @pl.when(z == last)
        def _():
            rank_copy(0).wait_recv()

        @pl.when(z > 0)
        def _():
            rank_sum[...] += rank_got[0, z].astype(F32)

        @pl.when(z == 0)
        def _():
            rank_copy(1).wait_recv()

        @pl.when(z < last)
        def _():
            rank_sum[...] += rank_got[1, z].astype(F32)

        spread = lax.dot_general(
            rank_sum[...].astype(BF16),
            rank_hot(),
            (((0,), (0,)), ((), ())),
            preferred_element_type=F32,
        )
        expanded = jnp.where(token_mask(z * rows, rows), spread, 0.0).astype(BF16)

        def own(block, carry):
            cols = pl.ds(pl.multiple_of(block * BLOCK_COLS, BLOCK_COLS), BLOCK_COLS)
            lora = jnp.dot(
                expanded,
                got_up[:, :, cols].reshape(lanes, BLOCK_COLS),
                preferred_element_type=F32,
            )
            total[block] = base_part(z, block).astype(F32) + ADAPTER_SCALE * lora
            return carry

        lax.fori_loop(0, blocks, own, 0)

    right_count = (last - z) * blocks
    left_count = z * blocks
    final_step = (tp_count - 2) * blocks + LAG

    rank_step = blocks + 1

    neighbours = jnp.where(z > 0, 1, 0) + jnp.where(z < last, 1, 0)
    tok_copy(first).wait()
    for i, (low, count) in enumerate(PIECES):
        cols = pl.ds(low, count)
        first_weight_copy(i).wait()

        @pl.when((z == 0) | (z == last))
        def _():
            part = jnp.dot(tok[first], weight[0, :, cols], preferred_element_type=F32)
            stage[first * blocks, :, cols] = part.astype(BF16)

        if i == 0:
            pl.semaphore_wait(barrier, neighbours + groups - 1)

        for way, end in enumerate((0, last)):

            @pl.when(z == end)
            def _():
                piece_copy(way, i).start()

    def step(s, carry):
        @pl.when((s > 0) & (s < blocks))
        def _():
            weight_copy(s).wait()

        @pl.when(s == 1)
        def _():
            tok_copy(last - first).wait()
            for chunk in range(1, last):
                tok_copy(chunk).wait()

        k_right = s - LAG * z

        @pl.when((k_right >= DEPTH) & (k_right < right_count + DEPTH))
        def _():
            @pl.when((z == 0) & (k_right == DEPTH))
            def _():
                for i in range(len(PIECES)):
                    piece_copy(0, i).wait_send()

            @pl.when((z != 0) | (k_right > DEPTH))
            def _():
                right_copy(k_right - DEPTH).wait_send()

        @pl.when((k_right >= 0) & (k_right < right_count))
        def _():
            chunk = last - k_right // blocks
            block = lax.rem(k_right, blocks)
            at = chunk * blocks + block

            @pl.when((z == 0) & (s > 0))
            def _():
                stage[at] = base_part(chunk, block)

            @pl.when(z > 0)
            def _():
                part = base_part(chunk, block)

                @pl.when((z == 1) & (k_right == 0))
                def _():
                    for i in range(len(PIECES)):
                        piece_copy(0, i).wait_recv()

                @pl.when((z != 1) | (k_right > 0))
                def _():
                    right_copy(k_right).wait_recv()

                stage[at] = (part.astype(F32) + from_left[k_right].astype(F32)).astype(BF16)

            @pl.when((z != 0) | (s > 0))
            def _():
                right_copy(k_right).start()

        k_left = s - LAG * (last - z)

        @pl.when((k_left >= DEPTH) & (k_left < left_count + DEPTH))
        def _():
            @pl.when((z == last) & (k_left == DEPTH))
            def _():
                for i in range(len(PIECES)):
                    piece_copy(1, i).wait_send()

            @pl.when((z != last) | (k_left > DEPTH))
            def _():
                left_copy(k_left - DEPTH).wait_send()

        @pl.when((k_left >= 0) & (k_left < left_count))
        def _():
            chunk = k_left // blocks
            block = lax.rem(k_left, blocks)

            @pl.when((z == last) & (s > 0))
            def _():
                stage[k_left] = base_part(chunk, block)

            @pl.when(z < last)
            def _():
                part = base_part(chunk, block)

                @pl.when((z == last - 1) & (k_left == 0))
                def _():
                    for i in range(len(PIECES)):
                        piece_copy(1, i).wait_recv()

                @pl.when((z != last - 1) | (k_left > 0))
                def _():
                    left_copy(k_left).wait_recv()

                stage[k_left] = (part.astype(F32) + from_right[k_left].astype(F32)).astype(BF16)

            @pl.when((z != last) | (s > 0))
            def _():
                left_copy(k_left).start()

        @pl.when(s == 1)
        def _():
            send_adapters()

        @pl.when(s == rank_step)
        def _():
            send_ranks()

        @pl.when((s == rank_step + z) & (z < last))
        def _():
            pass_ranks(0)

        @pl.when((s == rank_step + last - z) & (z > 0))
        def _():
            pass_ranks(1)

        @pl.when(s == final_step - 1)
        def _():
            expand_ranks()

        early = s - final_step + 1
        inner = (early >= 0) & (early < blocks) & (z > 0) & (z < last)

        @pl.when(inner & (2 * z < last))
        def _():
            left_copy(left_count + early).wait_recv()
            total[early] += from_right[left_count + early].astype(F32)

        @pl.when(inner & (2 * z >= last))
        def _():
            right_copy(right_count + early).wait_recv()
            total[early] += from_left[right_count + early].astype(F32)

        block = s - final_step
        own = (block >= 0) & (block < blocks)
        late_left = (z == 0) | ((2 * z >= last) & (z < last))
        cols = pl.ds(pl.multiple_of(block * BLOCK_COLS, BLOCK_COLS), BLOCK_COLS)

        @pl.when(own & late_left)
        def _():
            left_copy(left_count + block).wait_recv()
            late = from_right[left_count + block].astype(F32)
            out[:, cols] = (total[block] + late).astype(BF16)

        @pl.when(own & jnp.logical_not(late_left))
        def _():
            right_copy(right_count + block).wait_recv()
            late = from_left[right_count + block].astype(F32)
            out[:, cols] = (total[block] + late).astype(BF16)

        return carry

    lax.fori_loop(0, last * blocks + max(LAG, DEPTH), step, 0)

    @pl.when(z < last)
    def _():
        rank_copy(0).wait_send()

    @pl.when(z > 0)
    def _():
        rank_copy(1).wait_send()


def local(
    tokens,
    query_weight_matrix,
    adapter_down_weight,
    adapter_up_weight,
    request_adapter_id,
    request_token_length,
    adapter_store_slot,
):
    tp_count = lax.axis_size("tp")
    groups = lax.axis_size("ad")
    tok_rows, width = tokens.shape[1:]
    cols = query_weight_matrix.shape[1]
    held, rank_extent = adapter_down_weight.shape[:2]
    rows = tok_rows // tp_count
    blocks = cols // BLOCK_COLS
    cap_rows = CAP * rank_extent
    block = (rows, BLOCK_COLS)
    flow = (tp_count - 1) * blocks
    hbm = pl.BlockSpec(memory_space=pltpu.HBM)
    dma = pltpu.SemaphoreType.DMA
    query = pl.pallas_call(
        functools.partial(kernel, tp_count, groups, rank_extent),
        out_shape=pltpu.VMEM((rows, cols), BF16),
        in_specs=[hbm] * 7,
        out_specs=pl.BlockSpec(memory_space=pltpu.VMEM),
        scratch_shapes=[
            pltpu.VMEM((tp_count, rows, width), BF16),
            pltpu.VMEM((blocks, width, BLOCK_COLS), BF16),
            pltpu.VMEM((held * rank_extent, width), BF16),
            pltpu.VMEM((held * rank_extent, cols), BF16),
            pltpu.VMEM((tp_count * blocks, *block), BF16),
            pltpu.VMEM((flow, *block), BF16),
            pltpu.VMEM((flow, *block), BF16),
            pltpu.VMEM((groups - 1, cap_rows, width), BF16),
            pltpu.VMEM((groups - 1, cap_rows, cols), BF16),
            pltpu.VMEM((groups, cap_rows, width), BF16),
            pltpu.VMEM((groups, cap_rows, cols), BF16),
            pltpu.VMEM((tp_count, rank_extent, rows), BF16),
            pltpu.VMEM((2, tp_count, rank_extent, rows), BF16),
            pltpu.VMEM((2, tp_count, rank_extent, rows), BF16),
            pltpu.VMEM((rank_extent, rows), F32),
            pltpu.VMEM((blocks, *block), F32),
            pltpu.SMEM(request_adapter_id.shape, jnp.int32),
            pltpu.SMEM(request_token_length.shape, jnp.int32),
            pltpu.SMEM(adapter_store_slot.shape, jnp.int32),
            dma((tp_count,)),
            dma((blocks,)),
            dma((2,)),
            dma((3,)),
            dma((tp_count * blocks,)),
            dma((flow,)),
            dma((flow,)),
            dma((2, groups - 1)),
            dma((2, groups - 1)),
            dma((2,)),
            dma((2,)),
            dma((len(PIECES),)),
            dma((2, len(PIECES))),
            dma((2, len(PIECES))),
        ],
        compiler_params=pltpu.CompilerParams(
            collective_id=0, has_side_effects=True, vmem_limit_bytes=56 * 2**20
        ),
        cost_estimate=pl.CostEstimate(
            flops=2 * tok_rows * width * cols,
            bytes_accessed=2 * width * (cols + tok_rows),
            transcendentals=0,
        ),
        name="query_projection",
    )(
        tokens.reshape(tok_rows, width),
        query_weight_matrix,
        adapter_down_weight.reshape(held * rank_extent, width),
        adapter_up_weight.reshape(held * rank_extent, cols),
        request_adapter_id,
        request_token_length,
        adapter_store_slot,
    )
    return query[None]


def solution(mesh):
    return jax.shard_map(
        local,
        mesh=mesh,
        in_specs=(
            P(("rep", "ad"), None, "tp"),
            P("tp", "sub"),
            P("ad", None, "tp"),
            P("ad", None, "sub"),
            P("rep", None),
            P(("rep", "ad"), None),
            P("rep"),
        ),
        out_specs=P(("rep", "ad"), "tp", "sub"),
        check_vma=False,
    )
```

```python
import functools
import jax
import jax.numpy as jnp
from jax import lax
from jax.experimental import pallas as pl
from jax.experimental.pallas import tpu as pltpu
from jax.sharding import PartitionSpec as P

CAP = 4

ADAPTER_SCALE = 2.0

BLOCK_COLS = 512
PIECES = ((0, 128), (128, 128), (256, 256))
LAG = 3
DEPTH = 2

MESH = pl.DeviceIdType.MESH
F32 = jnp.float32
BF16 = jnp.bfloat16


def one_hot(condition):
    return jnp.where(condition, 1.0, 0.0).astype(BF16)


def kernel(
    tp_count,
    groups,
    rank_extent,
    tokens_hbm,
    weight_hbm,
    down_hbm,
    up_hbm,
    ids_hbm,
    lengths_hbm,
    slots_hbm,
    out,
    tok,
    weight,
    down,
    up,
    stage,
    from_left,
    from_right,
    down_send,
    up_send,
    got_down,
    got_up,
    rank_own,
    rank_send,
    rank_got,
    rank_sum,
    total,
    ids_ref,
    lengths_ref,
    slots_ref,
    tok_sem,
    weight_sem,
    store_sem,
    small_sem,
    flow_send_sem,
    left_sem,
    right_sem,
    adapter_send_sem,
    adapter_recv_sem,
    rank_send_sem,
    rank_recv_sem,
    piece_weight_sem,
    piece_send_sem,
    piece_recv_sem,
):
    z = lax.axis_index("tp")
    ad = lax.axis_index("ad")
    rows = tok.shape[1]
    blocks = weight.shape[0]
    requests = ids_ref.shape[1]
    store_rows = down.shape[0]
    held = store_rows // rank_extent
    cap_rows = CAP * rank_extent
    lanes = groups * cap_rows
    rank_bits = rank_extent.bit_length() - 1
    last = tp_count - 1

    def tok_copy(chunk):
        return pltpu.make_async_copy(
            tokens_hbm.at[pl.ds(chunk * rows, rows), :], tok.at[chunk], tok_sem.at[chunk]
        )

    def weight_copy(block):
        return pltpu.make_async_copy(
            weight_hbm.at[:, pl.ds(pl.multiple_of(block * BLOCK_COLS, BLOCK_COLS), BLOCK_COLS)],
            weight.at[block],
            weight_sem.at[block],
        )

    def first_weight_copy(i):
        cols = pl.ds(*PIECES[i])
        return pltpu.make_async_copy(
            weight_hbm.at[:, cols], weight.at[0, :, cols], piece_weight_sem.at[i]
        )

    down_copy = pltpu.make_async_copy(down_hbm, down, store_sem.at[0])
    up_copy = pltpu.make_async_copy(up_hbm, up, store_sem.at[1])
    small_copies = [
        pltpu.make_async_copy(source, target, small_sem.at[i])
        for i, (source, target) in enumerate(
            ((ids_hbm, ids_ref), (lengths_hbm, lengths_ref), (slots_hbm, slots_ref))
        )
    ]
    first = jnp.where(z == last, 0, last)
    first_weight_copy(0).start()
    tok_copy(first).start()

    barrier = pltpu.get_barrier_semaphore()

    def greet(target):
        pl.semaphore_signal(barrier, inc=1, device_id=target, device_id_type=MESH)

    @pl.when(z < last)
    def _():
        greet({"tp": lax.rem(z + 1, tp_count)})

    @pl.when(z > 0)
    def _():
        greet({"tp": lax.rem(z + last, tp_count)})

    for hop in range(1, groups):
        greet({"ad": lax.rem(ad + hop, groups)})

    for i in range(1, len(PIECES)):
        first_weight_copy(i).start()
    weight_copy(1).start()
    tok_copy(last - first).start()
    for chunk in range(1, last):
        tok_copy(chunk).start()
    for small in small_copies:
        small.start()
    down_copy.start()
    up_copy.start()
    for block in range(2, blocks):
        weight_copy(block).start()

    def right_copy(k):
        return pltpu.make_async_remote_copy(
            stage.at[last * blocks - k + 2 * lax.rem(k, blocks)],
            from_left.at[k],
            flow_send_sem.at[last * blocks - k + 2 * lax.rem(k, blocks)],
            left_sem.at[k],
            device_id={"tp": lax.rem(z + 1, tp_count)},
            device_id_type=MESH,
        )

    def left_copy(k):
        return pltpu.make_async_remote_copy(
            stage.at[k],
            from_right.at[k],
            flow_send_sem.at[k],
            right_sem.at[k],
            device_id={"tp": lax.rem(z + last, tp_count)},
            device_id_type=MESH,
        )

    def piece_copy(way, i):
        cols = pl.ds(*PIECES[i])
        got, at, hop = ((from_left, last * blocks, 1), (from_right, 0, last))[way]
        return pltpu.make_async_remote_copy(
            stage.at[at, :, cols],
            got.at[0, :, cols],
            piece_send_sem.at[way, i],
            piece_recv_sem.at[way, i],
            device_id={"tp": lax.rem(z + hop, tp_count)},
            device_id_type=MESH,
        )

    def base_part(chunk, block):
        part = jnp.dot(tok[chunk], weight[block], preferred_element_type=F32)
        return part.astype(BF16)

    def adapter_copy(which, hop):
        send, got = ((down_send, got_down), (up_send, got_up))[which]
        return pltpu.make_async_remote_copy(
            send.at[hop - 1],
            got.at[ad],
            adapter_send_sem.at[which, hop - 1],
            adapter_recv_sem.at[which, hop - 1],
            device_id={"ad": lax.rem(ad + hop, groups)},
            device_id_type=MESH,
        )

    def rank_copy(way):
        return pltpu.make_async_remote_copy(
            rank_send.at[way],
            rank_got.at[way],
            rank_send_sem.at[way],
            rank_recv_sem.at[way],
            device_id={"tp": lax.rem(z + (1 if way == 0 else last), tp_count)},
            device_id_type=MESH,
        )

    def places(group):
        found = []
        for q in range(requests):
            slot = slots_ref[ids_ref[group, q]]
            owner = jnp.int32(0)
            for g in range(1, groups):
                owner = owner + jnp.where(slot >= g * held, 1, 0)
            rank = jnp.int32(0)
            for earlier, _, _ in found:
                rank = rank + jnp.where(earlier == owner, 1, 0)
            found.append((owner, rank, slot - owner * held))
        return found

    def send_adapters():
        for small in small_copies:
            small.wait()
        down_copy.wait()
        up_copy.wait()
        row = lax.broadcasted_iota(jnp.int32, (cap_rows, store_rows), 0)
        col = lax.broadcasted_iota(jnp.int32, (cap_rows, store_rows), 1)
        for hop in list(range(1, groups)) + [0]:
            wanted = jnp.full((cap_rows, store_rows), -1 - rank_extent, jnp.int32)
            for owner, rank, within in places(lax.rem(ad + hop, groups)):
                place = jnp.where(owner == ad, rank, -1)
                wanted = jnp.where((row >> rank_bits) == place, within * rank_extent, wanted)
            chosen = one_hot(col == wanted + (row & (rank_extent - 1)))
            for which, (store, send, got) in enumerate(
                ((down, down_send, got_down), (up, up_send, got_up))
            ):
                picked = jnp.dot(chosen, store[...], preferred_element_type=F32).astype(BF16)
                if hop > 0:
                    send[hop - 1] = picked
                    adapter_copy(which, hop).start()
                else:
                    got[ad] = picked

    def token_mask(first, count):
        lane = lax.broadcasted_iota(jnp.int32, (1, lanes), 1) >> rank_bits
        starts = jnp.zeros((1, lanes), jnp.int32)
        ends = jnp.zeros((1, lanes), jnp.int32)
        position = jnp.int32(0)
        for q, (owner, rank, _) in enumerate(places(ad)):
            here = lane == owner * CAP + rank
            starts = jnp.where(here, position, starts)
            position = position + lengths_ref[0, q]
            ends = jnp.where(here, position, ends)
        at = first + lax.broadcasted_iota(jnp.int32, (count, lanes), 0)
        return (at >= starts) & (at < ends)

    def rank_hot():
        lane = lax.broadcasted_iota(jnp.int32, (rank_extent, lanes), 1)
        row = lax.broadcasted_iota(jnp.int32, (rank_extent, lanes), 0)
        return one_hot((lane & (rank_extent - 1)) == row)

    def send_ranks():
        for hop in range(1, groups):
            adapter_copy(0, hop).wait()
        acts = lax.dot_general(
            tok[...].reshape(tp_count * rows, -1),
            got_down[...].reshape(lanes, -1),
            (((1,), (1,)), ((), ())),
            preferred_element_type=F32,
        )
        acts = jnp.where(token_mask(0, tp_count * rows), acts, 0.0).astype(BF16)
        for chunk in range(tp_count):
            rank_own[chunk] = lax.dot_general(
                rank_hot(),
                acts[chunk * rows : (chunk + 1) * rows],
                (((1,), (1,)), ((), ())),
                preferred_element_type=F32,
            ).astype(BF16)

    def pass_ranks(way):
        @pl.when(z == (0 if way == 0 else last))
        def _():
            rank_send[way] = rank_own[...]

        @pl.when(z != (0 if way == 0 else last))
        def _():
            rank_copy(way).wait_recv()
            rank_send[way] = (rank_own[...].astype(F32) + rank_got[way].astype(F32)).astype(BF16)

        rank_copy(way).start()

    def expand_ranks():
        for hop in range(1, groups):
            adapter_copy(1, hop).wait()
        rank_sum[...] = rank_own[z].astype(F32)

        @pl.when(z == last)
        def _():
            rank_copy(0).wait_recv()

        @pl.when(z > 0)
        def _():
            rank_sum[...] += rank_got[0, z].astype(F32)

        @pl.when(z == 0)
        def _():
            rank_copy(1).wait_recv()

        @pl.when(z < last)
        def _():
            rank_sum[...] += rank_got[1, z].astype(F32)

        spread = lax.dot_general(
            rank_sum[...].astype(BF16),
            rank_hot(),
            (((0,), (0,)), ((), ())),
            preferred_element_type=F32,
        )
        expanded = jnp.where(token_mask(z * rows, rows), spread, 0.0).astype(BF16)

        def own(block, carry):
            cols = pl.ds(pl.multiple_of(block * BLOCK_COLS, BLOCK_COLS), BLOCK_COLS)
            lora = jnp.dot(
                expanded,
                got_up[:, :, cols].reshape(lanes, BLOCK_COLS),
                preferred_element_type=F32,
            )
            total[block] = base_part(z, block).astype(F32) + ADAPTER_SCALE * lora
            return carry

        lax.fori_loop(0, blocks, own, 0)

    right_count = (last - z) * blocks
    left_count = z * blocks
    final_step = (tp_count - 2) * blocks + LAG

    rank_step = blocks + 1

    neighbours = jnp.where(z > 0, 1, 0) + jnp.where(z < last, 1, 0)
    tok_copy(first).wait()
    for i, (low, count) in enumerate(PIECES):
        cols = pl.ds(low, count)
        first_weight_copy(i).wait()

        @pl.when((z == 0) | (z == last))
        def _():
            part = jnp.dot(tok[first], weight[0, :, cols], preferred_element_type=F32)
            stage[first * blocks, :, cols] = part.astype(BF16)

        if i == 0:
            pl.semaphore_wait(barrier, neighbours + groups - 1)

        for way, end in enumerate((0, last)):

            @pl.when(z == end)
            def _():
                piece_copy(way, i).start()

    def step(s, carry):
        @pl.when((s > 0) & (s < blocks))
        def _():
            weight_copy(s).wait()

        @pl.when(s == 1)
        def _():
            tok_copy(last - first).wait()
            for chunk in range(1, last):
                tok_copy(chunk).wait()

        k_right = s - LAG * z

        def right_sent():
            @pl.when((z == 0) & (k_right == DEPTH))
            def _():
                for i in range(len(PIECES)):
                    piece_copy(0, i).wait_send()

            @pl.when((z != 0) | (k_right > DEPTH))
            def _():
                right_copy(k_right - DEPTH).wait_send()

        @pl.when((k_right >= DEPTH) & (k_right >= right_count) & (k_right < right_count + DEPTH))
        def _():
            right_sent()

        @pl.when((k_right >= 0) & (k_right < right_count))
        def _():
            chunk = last - k_right // blocks
            block = lax.rem(k_right, blocks)
            at = chunk * blocks + block

            @pl.when((z == 0) & (s > 0))
            def _():
                stage[at] = base_part(chunk, block)

            @pl.when(z > 0)
            def _():
                part = base_part(chunk, block)

                @pl.when((z == 1) & (k_right == 0))
                def _():
                    for i in range(len(PIECES)):
                        piece_copy(0, i).wait_recv()

                @pl.when((z != 1) | (k_right > 0))
                def _():
                    right_copy(k_right).wait_recv()

                stage[at] = (part.astype(F32) + from_left[k_right].astype(F32)).astype(BF16)

            @pl.when(k_right >= DEPTH)
            def _():
                right_sent()

            @pl.when((z != 0) | (s > 0))
            def _():
                right_copy(k_right).start()

        k_left = s - LAG * (last - z)

        def left_sent():
            @pl.when((z == last) & (k_left == DEPTH))
            def _():
                for i in range(len(PIECES)):
                    piece_copy(1, i).wait_send()

            @pl.when((z != last) | (k_left > DEPTH))
            def _():
                left_copy(k_left - DEPTH).wait_send()

        @pl.when((k_left >= DEPTH) & (k_left >= left_count) & (k_left < left_count + DEPTH))
        def _():
            left_sent()

        @pl.when((k_left >= 0) & (k_left < left_count))
        def _():
            chunk = k_left // blocks
            block = lax.rem(k_left, blocks)

            @pl.when((z == last) & (s > 0))
            def _():
                stage[k_left] = base_part(chunk, block)

            @pl.when(z < last)
            def _():
                part = base_part(chunk, block)

                @pl.when((z == last - 1) & (k_left == 0))
                def _():
                    for i in range(len(PIECES)):
                        piece_copy(1, i).wait_recv()

                @pl.when((z != last - 1) | (k_left > 0))
                def _():
                    left_copy(k_left).wait_recv()

                stage[k_left] = (part.astype(F32) + from_right[k_left].astype(F32)).astype(BF16)

            @pl.when(k_left >= DEPTH)
            def _():
                left_sent()

            @pl.when((z != last) | (s > 0))
            def _():
                left_copy(k_left).start()

        @pl.when(s == 1)
        def _():
            send_adapters()

        @pl.when(s == rank_step)
        def _():
            send_ranks()

        @pl.when((s == rank_step + z) & (z < last))
        def _():
            pass_ranks(0)

        @pl.when((s == rank_step + last - z) & (z > 0))
        def _():
            pass_ranks(1)

        @pl.when(s == final_step - 1)
        def _():
            expand_ranks()

        early = s - final_step + 1
        inner = (early >= 0) & (early < blocks) & (z > 0) & (z < last)

        @pl.when(inner & (2 * z < last))
        def _():
            left_copy(left_count + early).wait_recv()
            total[early] += from_right[left_count + early].astype(F32)

        @pl.when(inner & (2 * z >= last))
        def _():
            right_copy(right_count + early).wait_recv()
            total[early] += from_left[right_count + early].astype(F32)

        block = s - final_step
        own = (block >= 0) & (block < blocks)
        late_left = (z == 0) | ((2 * z >= last) & (z < last))
        cols = pl.ds(pl.multiple_of(block * BLOCK_COLS, BLOCK_COLS), BLOCK_COLS)

        @pl.when(own & late_left)
        def _():
            left_copy(left_count + block).wait_recv()
            late = from_right[left_count + block].astype(F32)
            out[:, cols] = (total[block] + late).astype(BF16)

        @pl.when(own & jnp.logical_not(late_left))
        def _():
            right_copy(right_count + block).wait_recv()
            late = from_left[right_count + block].astype(F32)
            out[:, cols] = (total[block] + late).astype(BF16)

        return carry

    lax.fori_loop(0, last * blocks + max(LAG, DEPTH), step, 0)

    @pl.when(z < last)
    def _():
        rank_copy(0).wait_send()

    @pl.when(z > 0)
    def _():
        rank_copy(1).wait_send()


def local(
    tokens,
    query_weight_matrix,
    adapter_down_weight,
    adapter_up_weight,
    request_adapter_id,
    request_token_length,
    adapter_store_slot,
):
    tp_count = lax.axis_size("tp")
    groups = lax.axis_size("ad")
    tok_rows, width = tokens.shape[1:]
    cols = query_weight_matrix.shape[1]
    held, rank_extent = adapter_down_weight.shape[:2]
    rows = tok_rows // tp_count
    blocks = cols // BLOCK_COLS
    cap_rows = CAP * rank_extent
    block = (rows, BLOCK_COLS)
    flow = (tp_count - 1) * blocks
    hbm = pl.BlockSpec(memory_space=pltpu.HBM)
    dma = pltpu.SemaphoreType.DMA
    query = pl.pallas_call(
        functools.partial(kernel, tp_count, groups, rank_extent),
        out_shape=pltpu.VMEM((rows, cols), BF16),
        in_specs=[hbm] * 7,
        out_specs=pl.BlockSpec(memory_space=pltpu.VMEM),
        scratch_shapes=[
            pltpu.VMEM((tp_count, rows, width), BF16),
            pltpu.VMEM((blocks, width, BLOCK_COLS), BF16),
            pltpu.VMEM((held * rank_extent, width), BF16),
            pltpu.VMEM((held * rank_extent, cols), BF16),
            pltpu.VMEM((tp_count * blocks, *block), BF16),
            pltpu.VMEM((flow, *block), BF16),
            pltpu.VMEM((flow, *block), BF16),
            pltpu.VMEM((groups - 1, cap_rows, width), BF16),
            pltpu.VMEM((groups - 1, cap_rows, cols), BF16),
            pltpu.VMEM((groups, cap_rows, width), BF16),
            pltpu.VMEM((groups, cap_rows, cols), BF16),
            pltpu.VMEM((tp_count, rank_extent, rows), BF16),
            pltpu.VMEM((2, tp_count, rank_extent, rows), BF16),
            pltpu.VMEM((2, tp_count, rank_extent, rows), BF16),
            pltpu.VMEM((rank_extent, rows), F32),
            pltpu.VMEM((blocks, *block), F32),
            pltpu.SMEM(request_adapter_id.shape, jnp.int32),
            pltpu.SMEM(request_token_length.shape, jnp.int32),
            pltpu.SMEM(adapter_store_slot.shape, jnp.int32),
            dma((tp_count,)),
            dma((blocks,)),
            dma((2,)),
            dma((3,)),
            dma((tp_count * blocks,)),
            dma((flow,)),
            dma((flow,)),
            dma((2, groups - 1)),
            dma((2, groups - 1)),
            dma((2,)),
            dma((2,)),
            dma((len(PIECES),)),
            dma((2, len(PIECES))),
            dma((2, len(PIECES))),
        ],
        compiler_params=pltpu.CompilerParams(
            collective_id=0, has_side_effects=True, vmem_limit_bytes=56 * 2**20
        ),
        cost_estimate=pl.CostEstimate(
            flops=2 * tok_rows * width * cols,
            bytes_accessed=2 * width * (cols + tok_rows),
            transcendentals=0,
        ),
        name="query_projection",
    )(
        tokens.reshape(tok_rows, width),
        query_weight_matrix,
        adapter_down_weight.reshape(held * rank_extent, width),
        adapter_up_weight.reshape(held * rank_extent, cols),
        request_adapter_id,
        request_token_length,
        adapter_store_slot,
    )
    return query[None]


def solution(mesh):
    return jax.shard_map(
        local,
        mesh=mesh,
        in_specs=(
            P(("rep", "ad"), None, "tp"),
            P("tp", "sub"),
            P("ad", None, "tp"),
            P("ad", None, "sub"),
            P("rep", None),
            P(("rep", "ad"), None),
            P("rep"),
        ),
        out_specs=P(("rep", "ad"), "tp", "sub"),
        check_vma=False,
    )
```

```python
import functools
import jax
import jax.numpy as jnp
from jax import lax
from jax.experimental import pallas as pl
from jax.experimental.pallas import tpu as pltpu
from jax.sharding import PartitionSpec as P

CAP = 4

ADAPTER_SCALE = 2.0

BLOCK_COLS = 512
PIECES = ((0, 128), (128, 128), (256, 256))
LAG = 3
DEPTH = 3

MESH = pl.DeviceIdType.MESH
F32 = jnp.float32
BF16 = jnp.bfloat16


def one_hot(condition):
    return jnp.where(condition, 1.0, 0.0).astype(BF16)


def kernel(
    tp_count,
    groups,
    rank_extent,
    tokens_hbm,
    weight_hbm,
    down_hbm,
    up_hbm,
    ids_hbm,
    lengths_hbm,
    slots_hbm,
    out,
    tok,
    weight,
    down,
    up,
    stage,
    from_left,
    from_right,
    down_send,
    up_send,
    got_down,
    got_up,
    rank_own,
    rank_send,
    rank_got,
    rank_sum,
    total,
    ids_ref,
    lengths_ref,
    slots_ref,
    tok_sem,
    weight_sem,
    store_sem,
    small_sem,
    flow_send_sem,
    left_sem,
    right_sem,
    adapter_send_sem,
    adapter_recv_sem,
    rank_send_sem,
    rank_recv_sem,
    piece_weight_sem,
    piece_send_sem,
    piece_recv_sem,
):
    z = lax.axis_index("tp")
    ad = lax.axis_index("ad")
    rows = tok.shape[1]
    blocks = weight.shape[0]
    requests = ids_ref.shape[1]
    store_rows = down.shape[0]
    held = store_rows // rank_extent
    cap_rows = CAP * rank_extent
    lanes = groups * cap_rows
    rank_bits = rank_extent.bit_length() - 1
    last = tp_count - 1

    def tok_copy(chunk):
        return pltpu.make_async_copy(
            tokens_hbm.at[pl.ds(chunk * rows, rows), :], tok.at[chunk], tok_sem.at[chunk]
        )

    def weight_copy(block):
        return pltpu.make_async_copy(
            weight_hbm.at[:, pl.ds(pl.multiple_of(block * BLOCK_COLS, BLOCK_COLS), BLOCK_COLS)],
            weight.at[block],
            weight_sem.at[block],
        )

    def first_weight_copy(i):
        cols = pl.ds(*PIECES[i])
        return pltpu.make_async_copy(
            weight_hbm.at[:, cols], weight.at[0, :, cols], piece_weight_sem.at[i]
        )

    down_copy = pltpu.make_async_copy(down_hbm, down, store_sem.at[0])
    up_copy = pltpu.make_async_copy(up_hbm, up, store_sem.at[1])
    small_copies = [
        pltpu.make_async_copy(source, target, small_sem.at[i])
        for i, (source, target) in enumerate(
            ((ids_hbm, ids_ref), (lengths_hbm, lengths_ref), (slots_hbm, slots_ref))
        )
    ]
    first = jnp.where(z == last, 0, last)
    first_weight_copy(0).start()
    tok_copy(first).start()

    barrier = pltpu.get_barrier_semaphore()

    def greet(target):
        pl.semaphore_signal(barrier, inc=1, device_id=target, device_id_type=MESH)

    @pl.when(z < last)
    def _():
        greet({"tp": lax.rem(z + 1, tp_count)})

    @pl.when(z > 0)
    def _():
        greet({"tp": lax.rem(z + last, tp_count)})

    for hop in range(1, groups):
        greet({"ad": lax.rem(ad + hop, groups)})

    for i in range(1, len(PIECES)):
        first_weight_copy(i).start()
    weight_copy(1).start()
    tok_copy(last - first).start()
    for chunk in range(1, last):
        tok_copy(chunk).start()
    for small in small_copies:
        small.start()
    down_copy.start()
    up_copy.start()
    for block in range(2, blocks):
        weight_copy(block).start()

    def right_copy(k):
        return pltpu.make_async_remote_copy(
            stage.at[last * blocks - k + 2 * lax.rem(k, blocks)],
            from_left.at[k],
            flow_send_sem.at[last * blocks - k + 2 * lax.rem(k, blocks)],
            left_sem.at[k],
            device_id={"tp": lax.rem(z + 1, tp_count)},
            device_id_type=MESH,
        )

    def left_copy(k):
        return pltpu.make_async_remote_copy(
            stage.at[k],
            from_right.at[k],
            flow_send_sem.at[k],
            right_sem.at[k],
            device_id={"tp": lax.rem(z + last, tp_count)},
            device_id_type=MESH,
        )

    def piece_copy(way, i):
        cols = pl.ds(*PIECES[i])
        got, at, hop = ((from_left, last * blocks, 1), (from_right, 0, last))[way]
        return pltpu.make_async_remote_copy(
            stage.at[at, :, cols],
            got.at[0, :, cols],
            piece_send_sem.at[way, i],
            piece_recv_sem.at[way, i],
            device_id={"tp": lax.rem(z + hop, tp_count)},
            device_id_type=MESH,
        )

    def base_part(chunk, block):
        part = jnp.dot(tok[chunk], weight[block], preferred_element_type=F32)
        return part.astype(BF16)

    def adapter_copy(which, hop):
        send, got = ((down_send, got_down), (up_send, got_up))[which]
        return pltpu.make_async_remote_copy(
            send.at[hop - 1],
            got.at[ad],
            adapter_send_sem.at[which, hop - 1],
            adapter_recv_sem.at[which, hop - 1],
            device_id={"ad": lax.rem(ad + hop, groups)},
            device_id_type=MESH,
        )

    def rank_copy(way):
        return pltpu.make_async_remote_copy(
            rank_send.at[way],
            rank_got.at[way],
            rank_send_sem.at[way],
            rank_recv_sem.at[way],
            device_id={"tp": lax.rem(z + (1 if way == 0 else last), tp_count)},
            device_id_type=MESH,
        )

    def places(group):
        found = []
        for q in range(requests):
            slot = slots_ref[ids_ref[group, q]]
            owner = jnp.int32(0)
            for g in range(1, groups):
                owner = owner + jnp.where(slot >= g * held, 1, 0)
            rank = jnp.int32(0)
            for earlier, _, _ in found:
                rank = rank + jnp.where(earlier == owner, 1, 0)
            found.append((owner, rank, slot - owner * held))
        return found

    def send_adapters():
        for small in small_copies:
            small.wait()
        down_copy.wait()
        up_copy.wait()
        row = lax.broadcasted_iota(jnp.int32, (cap_rows, store_rows), 0)
        col = lax.broadcasted_iota(jnp.int32, (cap_rows, store_rows), 1)
        for hop in list(range(1, groups)) + [0]:
            wanted = jnp.full((cap_rows, store_rows), -1 - rank_extent, jnp.int32)
            for owner, rank, within in places(lax.rem(ad + hop, groups)):
                place = jnp.where(owner == ad, rank, -1)
                wanted = jnp.where((row >> rank_bits) == place, within * rank_extent, wanted)
            chosen = one_hot(col == wanted + (row & (rank_extent - 1)))
            for which, (store, send, got) in enumerate(
                ((down, down_send, got_down), (up, up_send, got_up))
            ):
                picked = jnp.dot(chosen, store[...], preferred_element_type=F32).astype(BF16)
                if hop > 0:
                    send[hop - 1] = picked
                    adapter_copy(which, hop).start()
                else:
                    got[ad] = picked

    def token_mask(first, count):
        lane = lax.broadcasted_iota(jnp.int32, (1, lanes), 1) >> rank_bits
        starts = jnp.zeros((1, lanes), jnp.int32)
        ends = jnp.zeros((1, lanes), jnp.int32)
        position = jnp.int32(0)
        for q, (owner, rank, _) in enumerate(places(ad)):
            here = lane == owner * CAP + rank
            starts = jnp.where(here, position, starts)
            position = position + lengths_ref[0, q]
            ends = jnp.where(here, position, ends)
        at = first + lax.broadcasted_iota(jnp.int32, (count, lanes), 0)
        return (at >= starts) & (at < ends)

    def rank_hot():
        lane = lax.broadcasted_iota(jnp.int32, (rank_extent, lanes), 1)
        row = lax.broadcasted_iota(jnp.int32, (rank_extent, lanes), 0)
        return one_hot((lane & (rank_extent - 1)) == row)

    def send_ranks():
        for hop in range(1, groups):
            adapter_copy(0, hop).wait()
        acts = lax.dot_general(
            tok[...].reshape(tp_count * rows, -1),
            got_down[...].reshape(lanes, -1),
            (((1,), (1,)), ((), ())),
            preferred_element_type=F32,
        )
        acts = jnp.where(token_mask(0, tp_count * rows), acts, 0.0).astype(BF16)
        for chunk in range(tp_count):
            rank_own[chunk] = lax.dot_general(
                rank_hot(),
                acts[chunk * rows : (chunk + 1) * rows],
                (((1,), (1,)), ((), ())),
                preferred_element_type=F32,
            ).astype(BF16)

    def pass_ranks(way):
        @pl.when(z == (0 if way == 0 else last))
        def _():
            rank_send[way] = rank_own[...]

        @pl.when(z != (0 if way == 0 else last))
        def _():
            rank_copy(way).wait_recv()
            rank_send[way] = (rank_own[...].astype(F32) + rank_got[way].astype(F32)).astype(BF16)

        rank_copy(way).start()

    def expand_ranks():
        for hop in range(1, groups):
            adapter_copy(1, hop).wait()
        rank_sum[...] = rank_own[z].astype(F32)

        @pl.when(z == last)
        def _():
            rank_copy(0).wait_recv()

        @pl.when(z > 0)
        def _():
            rank_sum[...] += rank_got[0, z].astype(F32)

        @pl.when(z == 0)
        def _():
            rank_copy(1).wait_recv()

        @pl.when(z < last)
        def _():
            rank_sum[...] += rank_got[1, z].astype(F32)

        spread = lax.dot_general(
            rank_sum[...].astype(BF16),
            rank_hot(),
            (((0,), (0,)), ((), ())),
            preferred_element_type=F32,
        )
        expanded = jnp.where(token_mask(z * rows, rows), spread, 0.0).astype(BF16)

        def own(block, carry):
            cols = pl.ds(pl.multiple_of(block * BLOCK_COLS, BLOCK_COLS), BLOCK_COLS)
            lora = jnp.dot(
                expanded,
                got_up[:, :, cols].reshape(lanes, BLOCK_COLS),
                preferred_element_type=F32,
            )
            total[block] = base_part(z, block).astype(F32) + ADAPTER_SCALE * lora
            return carry

        lax.fori_loop(0, blocks, own, 0)

    right_count = (last - z) * blocks
    left_count = z * blocks
    final_step = (tp_count - 2) * blocks + LAG

    rank_step = blocks + 1

    neighbours = jnp.where(z > 0, 1, 0) + jnp.where(z < last, 1, 0)
    tok_copy(first).wait()
    for i, (low, count) in enumerate(PIECES):
        cols = pl.ds(low, count)
        first_weight_copy(i).wait()

        @pl.when((z == 0) | (z == last))
        def _():
            part = jnp.dot(tok[first], weight[0, :, cols], preferred_element_type=F32)
            stage[first * blocks, :, cols] = part.astype(BF16)

        if i == 0:
            pl.semaphore_wait(barrier, neighbours + groups - 1)

        for way, end in enumerate((0, last)):

            @pl.when(z == end)
            def _():
                piece_copy(way, i).start()

    def step(s, carry):
        @pl.when((s > 0) & (s < blocks))
        def _():
            weight_copy(s).wait()

        @pl.when(s == 1)
        def _():
            tok_copy(last - first).wait()
            for chunk in range(1, last):
                tok_copy(chunk).wait()

        k_right = s - LAG * z

        def right_sent():
            @pl.when((z == 0) & (k_right == DEPTH))
            def _():
                for i in range(len(PIECES)):
                    piece_copy(0, i).wait_send()

            @pl.when((z != 0) | (k_right > DEPTH))
            def _():
                right_copy(k_right - DEPTH).wait_send()

        @pl.when((k_right >= DEPTH) & (k_right >= right_count) & (k_right < right_count + DEPTH))
        def _():
            right_sent()

        @pl.when((k_right >= 0) & (k_right < right_count))
        def _():
            chunk = last - k_right // blocks
            block = lax.rem(k_right, blocks)
            at = chunk * blocks + block

            @pl.when((z == 0) & (s > 0))
            def _():
                stage[at] = base_part(chunk, block)

            @pl.when(z > 0)
            def _():
                part = base_part(chunk, block)

                @pl.when((z == 1) & (k_right == 0))
                def _():
                    for i in range(len(PIECES)):
                        piece_copy(0, i).wait_recv()

                @pl.when((z != 1) | (k_right > 0))
                def _():
                    right_copy(k_right).wait_recv()

                stage[at] = (part.astype(F32) + from_left[k_right].astype(F32)).astype(BF16)

            @pl.when(k_right >= DEPTH)
            def _():
                right_sent()

            @pl.when((z != 0) | (s > 0))
            def _():
                right_copy(k_right).start()

        k_left = s - LAG * (last - z)

        def left_sent():
            @pl.when((z == last) & (k_left == DEPTH))
            def _():
                for i in range(len(PIECES)):
                    piece_copy(1, i).wait_send()

            @pl.when((z != last) | (k_left > DEPTH))
            def _():
                left_copy(k_left - DEPTH).wait_send()

        @pl.when((k_left >= DEPTH) & (k_left >= left_count) & (k_left < left_count + DEPTH))
        def _():
            left_sent()

        @pl.when((k_left >= 0) & (k_left < left_count))
        def _():
            chunk = k_left // blocks
            block = lax.rem(k_left, blocks)

            @pl.when((z == last) & (s > 0))
            def _():
                stage[k_left] = base_part(chunk, block)

            @pl.when(z < last)
            def _():
                part = base_part(chunk, block)

                @pl.when((z == last - 1) & (k_left == 0))
                def _():
                    for i in range(len(PIECES)):
                        piece_copy(1, i).wait_recv()

                @pl.when((z != last - 1) | (k_left > 0))
                def _():
                    left_copy(k_left).wait_recv()

                stage[k_left] = (part.astype(F32) + from_right[k_left].astype(F32)).astype(BF16)

            @pl.when(k_left >= DEPTH)
            def _():
                left_sent()

            @pl.when((z != last) | (s > 0))
            def _():
                left_copy(k_left).start()

        @pl.when(s == 1)
        def _():
            send_adapters()

        @pl.when(s == rank_step)
        def _():
            send_ranks()

        @pl.when((s == rank_step + z) & (z < last))
        def _():
            pass_ranks(0)

        @pl.when((s == rank_step + last - z) & (z > 0))
        def _():
            pass_ranks(1)

        @pl.when(s == final_step - 1)
        def _():
            expand_ranks()

        early = s - final_step + 1
        inner = (early >= 0) & (early < blocks) & (z > 0) & (z < last)

        @pl.when(inner & (2 * z < last))
        def _():
            left_copy(left_count + early).wait_recv()
            total[early] += from_right[left_count + early].astype(F32)

        @pl.when(inner & (2 * z >= last))
        def _():
            right_copy(right_count + early).wait_recv()
            total[early] += from_left[right_count + early].astype(F32)

        block = s - final_step
        own = (block >= 0) & (block < blocks)
        late_left = (z == 0) | ((2 * z >= last) & (z < last))
        cols = pl.ds(pl.multiple_of(block * BLOCK_COLS, BLOCK_COLS), BLOCK_COLS)

        @pl.when(own & late_left)
        def _():
            left_copy(left_count + block).wait_recv()
            late = from_right[left_count + block].astype(F32)
            out[:, cols] = (total[block] + late).astype(BF16)

        @pl.when(own & jnp.logical_not(late_left))
        def _():
            right_copy(right_count + block).wait_recv()
            late = from_left[right_count + block].astype(F32)
            out[:, cols] = (total[block] + late).astype(BF16)

        return carry

    lax.fori_loop(0, last * blocks + max(LAG, DEPTH), step, 0)

    @pl.when(z < last)
    def _():
        rank_copy(0).wait_send()

    @pl.when(z > 0)
    def _():
        rank_copy(1).wait_send()


def local(
    tokens,
    query_weight_matrix,
    adapter_down_weight,
    adapter_up_weight,
    request_adapter_id,
    request_token_length,
    adapter_store_slot,
):
    tp_count = lax.axis_size("tp")
    groups = lax.axis_size("ad")
    tok_rows, width = tokens.shape[1:]
    cols = query_weight_matrix.shape[1]
    held, rank_extent = adapter_down_weight.shape[:2]
    rows = tok_rows // tp_count
    blocks = cols // BLOCK_COLS
    cap_rows = CAP * rank_extent
    block = (rows, BLOCK_COLS)
    flow = (tp_count - 1) * blocks
    hbm = pl.BlockSpec(memory_space=pltpu.HBM)
    dma = pltpu.SemaphoreType.DMA
    query = pl.pallas_call(
        functools.partial(kernel, tp_count, groups, rank_extent),
        out_shape=pltpu.VMEM((rows, cols), BF16),
        in_specs=[hbm] * 7,
        out_specs=pl.BlockSpec(memory_space=pltpu.VMEM),
        scratch_shapes=[
            pltpu.VMEM((tp_count, rows, width), BF16),
            pltpu.VMEM((blocks, width, BLOCK_COLS), BF16),
            pltpu.VMEM((held * rank_extent, width), BF16),
            pltpu.VMEM((held * rank_extent, cols), BF16),
            pltpu.VMEM((tp_count * blocks, *block), BF16),
            pltpu.VMEM((flow, *block), BF16),
            pltpu.VMEM((flow, *block), BF16),
            pltpu.VMEM((groups - 1, cap_rows, width), BF16),
            pltpu.VMEM((groups - 1, cap_rows, cols), BF16),
            pltpu.VMEM((groups, cap_rows, width), BF16),
            pltpu.VMEM((groups, cap_rows, cols), BF16),
            pltpu.VMEM((tp_count, rank_extent, rows), BF16),
            pltpu.VMEM((2, tp_count, rank_extent, rows), BF16),
            pltpu.VMEM((2, tp_count, rank_extent, rows), BF16),
            pltpu.VMEM((rank_extent, rows), F32),
            pltpu.VMEM((blocks, *block), F32),
            pltpu.SMEM(request_adapter_id.shape, jnp.int32),
            pltpu.SMEM(request_token_length.shape, jnp.int32),
            pltpu.SMEM(adapter_store_slot.shape, jnp.int32),
            dma((tp_count,)),
            dma((blocks,)),
            dma((2,)),
            dma((3,)),
            dma((tp_count * blocks,)),
            dma((flow,)),
            dma((flow,)),
            dma((2, groups - 1)),
            dma((2, groups - 1)),
            dma((2,)),
            dma((2,)),
            dma((len(PIECES),)),
            dma((2, len(PIECES))),
            dma((2, len(PIECES))),
        ],
        compiler_params=pltpu.CompilerParams(
            collective_id=0, has_side_effects=True, vmem_limit_bytes=56 * 2**20
        ),
        cost_estimate=pl.CostEstimate(
            flops=2 * tok_rows * width * cols,
            bytes_accessed=2 * width * (cols + tok_rows),
            transcendentals=0,
        ),
        name="query_projection",
    )(
        tokens.reshape(tok_rows, width),
        query_weight_matrix,
        adapter_down_weight.reshape(held * rank_extent, width),
        adapter_up_weight.reshape(held * rank_extent, cols),
        request_adapter_id,
        request_token_length,
        adapter_store_slot,
    )
    return query[None]


def solution(mesh):
    return jax.shard_map(
        local,
        mesh=mesh,
        in_specs=(
            P(("rep", "ad"), None, "tp"),
            P("tp", "sub"),
            P("ad", None, "tp"),
            P("ad", None, "sub"),
            P("rep", None),
            P(("rep", "ad"), None),
            P("rep"),
        ),
        out_specs=P(("rep", "ad"), "tp", "sub"),
        check_vma=False,
    )
```
